128 devices in a mesh: tile: 8 (over y, core), head: 16 (over z, x).
Axes of the slice: x: 4, y: 4, z: 4, core: 2. Of those that a mesh axis runs over, the one named last changes fastest.
Arguments:
- feature_map: bfloat16 [256, 512, 256], P('tile', 'head'), may hold values from -6 to 6
- fpn_weight: bfloat16 [3, 3, 256, 256], replicated, may hold values from -0.125 to 0.125
- head_weight: bfloat16 [16, 3, 3, 256, 256], P('head'), may hold values from -0.125 to 0.125
- deconv_weight: bfloat16 [16, 2, 2, 256, 256], P('head'), may hold values from -0.375 to 0.375
- mask_weight: bfloat16 [16, 256], P('head'), may hold values from -4 to 4
- box_class: int32 [2048], P(('tile', 'head')), may hold values from 0 to 15, as said below
- box_offset: int32 [2048, 2], P(('tile', 'head')), may hold values from 0 to 18
- valid_count: int32 [128], P(('tile', 'head')), may hold values from 12 to 16
- mask_cotangent: float32 [2048, 28, 28], P(('tile', 'head')), may hold values from -6 to 6
Outputs:
- grad_input: bfloat16 [256, 512, 256], P('tile', 'head')
- grad_fpn_weight: float32 [3, 3, 256, 256], replicated
The draws below stay inside these ranges and needn't reach their ends.
Inputs may be any that keep to these rules, and one draw needn't show every extreme that they name: `box_class`: among the slots of one device no class appears more than 2 times; in each row of tiles along tile one class is named by exactly 2 valid slots of every device of that row.
All inputs are finite; a program needn't handle non-finite values.
Results may differ from the reference program's by a relative error of at most 0.023.
Values may be sent and summed in bfloat16 or wider, within the bound.
A program may use at most 128 MiB of HBM per device.

```python
import jax
import jax.numpy as jnp
from jax import lax

C = 256
TILE = 32
R_DEV = 16
CLASSES = 16
H = 256
W = 512
BOXES = 2048
N_HEAD = 16


def box_plan(key):
    base = jax.random.fold_in(key, 7)
    devices = BOXES // R_DEV
    groups = devices // CLASSES
    key_hot, key_rest, key_order, key_count, key_full = jax.random.split(base, 5)
    hot = jax.random.randint(key_hot, (groups,), 0, CLASSES)
    hot_dev = jnp.repeat(hot, CLASSES)
    pairs = jnp.repeat(jnp.arange(1, CLASSES, dtype=jnp.int32), 2)
    others = jax.vmap(lambda part_key: jax.random.permutation(part_key, pairs)[:R_DEV - 2])(jax.random.split(key_rest, devices))
    plan = jnp.concatenate([jnp.stack([hot_dev, hot_dev], 1), (hot_dev[:, None] + others) % CLASSES], 1)
    order = jax.vmap(lambda part_key: jax.random.permutation(part_key, R_DEV))(jax.random.split(key_order, devices))
    classes = jnp.take_along_axis(plan, order, axis=1)
    last_hot = jnp.max(jnp.where(order < 2, jnp.arange(R_DEV)[None, :], 0), axis=1)
    counts = jax.random.randint(key_count, (devices,), R_DEV - R_DEV // 4, R_DEV + 1)
    counts = jnp.maximum(counts, last_hot + 1)
    chosen = jax.random.randint(key_full, (), 0, devices)
    counts = jnp.where(jnp.arange(devices) == chosen, R_DEV, counts)
    return (classes.reshape(-1).astype(jnp.int32), counts.astype(jnp.int32))


def draw_box_class(key, part):
    return box_plan(key)[0]


def draw_valid_count(key, part):
    return box_plan(key)[1]


def with_ends(values, rng, low, largest):
    extent = values.shape
    place = [jax.random.randint(jax.random.fold_in(rng, axis), (), 0, extent[axis]) for axis in range(len(extent))]
    values = values.at[tuple(place)].set(low)
    longest = extent.index(max(extent))
    place[longest] = (place[longest] + 1) % extent[longest]
    return values.at[tuple(place)].set(largest)


def block_scale(stream_key, dims, cuts, least, largest):
    loudness, own = 1.0, jax.random.fold_in(stream_key, 6)
    for axis_at, blocks in cuts:
        heights = jnp.exp(jax.random.uniform(jax.random.fold_in(own, axis_at), (blocks,), jnp.float32, least / len(cuts), largest / len(cuts)))
        loudness = loudness * jnp.repeat(heights, dims[axis_at] // blocks).reshape([-1 if axis == axis_at else 1 for axis in range(len(dims))])
    return loudness


def centred(key, extent, width, reach, cuts=(), kind=jnp.bfloat16):
    entries = jax.random.normal(key, extent, jnp.float32) * width
    if len(cuts) > 0:
        entries = block_scale(key, extent, cuts, -0.22, 0.18) * entries
    return jnp.clip(entries, min=-reach, max=reach).astype(kind)


def setup_inputs(seed: int = 0) -> dict:
    arg_keys = jax.random.split(jax.random.key(seed), 10)
    feature_map = centred(arg_keys[0], (H, W, C), 1.0, 6.0, ((0, 8), (1, 16)))
    fpn_weight = centred(arg_keys[1], (3, 3, C, C), (9 * C) ** -0.5, 0.125)
    head_weight = centred(arg_keys[2], (CLASSES, 3, 3, C, C), (9 * C) ** -0.5, 0.125, ((0, 16),))
    deconv_weight = centred(arg_keys[3], (CLASSES, 2, 2, C, C), C ** -0.5, 0.375, ((0, 16),))
    mask_weight = centred(arg_keys[4], (CLASSES, C), 1.0, 4.0, ((0, 16),))
    box_class = draw_box_class(jax.random.fold_in(arg_keys[9], 71), 0)
    box_offset = with_ends(jax.random.randint(arg_keys[6], (BOXES, 2), 0, TILE - 13), jax.random.fold_in(arg_keys[6], 1), 0, (TILE - 13) - 1).astype(jnp.int32)
    valid_count = draw_valid_count(jax.random.fold_in(arg_keys[9], 71), 0)
    mask_cotangent = centred(arg_keys[8], (BOXES, 28, 28), 1.0, 6.0, ((0, 128),), jnp.float32)
    return {"feature_map": feature_map, "fpn_weight": fpn_weight, "head_weight": head_weight, "deconv_weight": deconv_weight, "mask_weight": mask_weight, "box_class": box_class, "box_offset": box_offset, "valid_count": valid_count, "mask_cotangent": mask_cotangent}


def conv_same(images, kernel):
    return lax.conv_general_dilated(images, kernel, (1, 1), 'SAME', dimension_numbers=('NHWC', 'HWIO', 'NHWC'), preferred_element_type=jnp.float32)

def flip_kernel(kernel):
    return jnp.transpose(kernel[::-1, ::-1], (0, 1, 3, 2))

def gelu_slope(value):
    cdf = 0.5 * (1.0 + lax.erf(value * 0.7071067811865476))
    dens = jnp.exp(-0.5 * value * value) * 0.3989422804014327
    return cdf + value * dens

def head_grad(blocks, cotangent, w_head, w_deconv, w_mask):
    count = blocks.shape[0]
    chans = blocks.shape[3]
    pre_one = conv_same(blocks, w_head)
    hidden = jax.nn.gelu(pre_one, approximate=False).astype(jnp.bfloat16)
    pre_two = jnp.einsum('nijk,abko->niajbo', hidden.astype(jnp.float32), w_deconv.astype(jnp.float32)).reshape(count, 28, 28, chans)
    upper = cotangent[..., None] * w_mask.astype(jnp.float32)
    dpre_two = (upper * gelu_slope(pre_two)).astype(jnp.bfloat16).reshape(count, 14, 2, 14, 2, chans)
    lower = jnp.einsum('niajbo,abko->nijk', dpre_two.astype(jnp.float32), w_deconv.astype(jnp.float32))
    dpre_one = (lower * gelu_slope(pre_one)).astype(jnp.bfloat16)
    return conv_same(dpre_one, flip_kernel(w_head)).astype(jnp.bfloat16)

def reference(feature_map, fpn_weight, head_weight, deconv_weight, mask_weight, box_class, box_offset, valid_count, mask_cotangent):
    chans = feature_map.shape[2]
    pyramid = conv_same(feature_map[None], fpn_weight)[0].astype(jnp.bfloat16)
    zero_index = jnp.zeros((), jnp.int32)

    def visit(grad_map, index):
        device = index // R_DEV
        slot = index % R_DEV
        row_start = device // N_HEAD * TILE + box_offset[index, 0]
        col_start = device % N_HEAD * TILE + box_offset[index, 1]

        def active(current):
            block = lax.dynamic_slice(pyramid, (row_start, col_start, zero_index), (14, 14, chans))
            klass = box_class[index]
            dblock = head_grad(block[None], mask_cotangent[index][None], head_weight[klass], deconv_weight[klass], mask_weight[klass])[0]
            patch = lax.dynamic_slice(current, (row_start, col_start, zero_index), (14, 14, chans))
            return lax.dynamic_update_slice(current, patch + dblock.astype(jnp.float32), (row_start, col_start, zero_index))
        return (lax.cond(slot < valid_count[device], active, lambda current: current, grad_map), None)
    start_map = jnp.zeros(pyramid.shape, jnp.float32)
    grad_map, _ = lax.scan(visit, start_map, jnp.arange(BOXES, dtype=jnp.int32))
    grad_pyramid = grad_map.astype(jnp.bfloat16)
    grad_input = conv_same(grad_pyramid[None], flip_kernel(fpn_weight))[0].astype(jnp.bfloat16)
    framed = jnp.pad(feature_map, ((1, 1), (1, 1), (0, 0)))
    flat_grad = grad_pyramid.reshape(-1, chans)
    pieces = []
    for shift_row in range(3):
        for shift_col in range(3):
            window = framed[shift_row:shift_row + H, shift_col:shift_col + W].reshape(-1, chans)
            pieces.append(lax.dot_general(window, flat_grad, (((0,), (0,)), ((), ())), preferred_element_type=jnp.float32))
    grad_fpn_weight = jnp.stack(pieces).reshape(3, 3, chans, chans) / BOXES
    return (grad_input, grad_fpn_weight)
```

```python
import functools

import jax
import jax.numpy as jnp
from jax import lax
from jax.experimental import pallas as pl
from jax.experimental.pallas import tpu as pltpu
from jax.sharding import PartitionSpec as P

MESH = pl.DeviceIdType.MESH
F32 = jnp.float32
BF16 = jnp.bfloat16

C = 256
HALF = 1680
ROWS = 2 * HALF
PIECES = ((0, 416), (416, 416), (832, 416), (1248, 432))
LAG = 2
SLOTS = (
    (0, 0), (3, 0), (1, 0), (1, 3), (3, 1), (0, 1), (0, 3), (1, 1),
    (3, 3), (0, 2), (2, 0), (3, 2), (2, 3), (1, 2), (2, 1), (2, 2),
)
DIRS = ("x+", "x-", "z+", "z-")
TOTAL = 2048


def plan():
    def hop(d, plus):
        if d == 1:
            return 0, "+"
        if d == 3:
            return 0, "-"
        return (1, "+") if plus else (3, "-")

    left = {d: [] for d in DIRS}
    for q in range(4):
        plus = q % 2 == 0
        for slot in SLOTS[1:]:
            dz, dx = slot
            if (dz if q < 2 else not dx):
                before, sign = hop(dz, plus)
                left["z" + sign].append((q, (before, dx), slot))
            else:
                before, sign = hop(dx, plus)
                left["x" + sign].append((q, (dz, before), slot))
    rank = {s: i for i, s in enumerate(SLOTS)}
    ready = {(q, (0, 0)): 0 for q in range(4)}
    sends = []
    while any(left.values()):
        step = len(sends)
        now = []
        for d in DIRS:
            can = [e for e in left[d] if ready.get((e[0], e[1]), 99) <= step]
            if can:
                e = min(can, key=lambda e: rank[e[2]])
                left[d].remove(e)
                ready[(e[0], e[2])] = step + LAG
                now.append((DIRS.index(d), e[0], rank[e[1]], rank[e[2]]))
        sends.append(now)
    whole = [0] + [max(ready[(q, s)] for q in range(4)) for s in SLOTS[1:]]
    first = max(w + 1 - i for i, w in enumerate(whole))
    return sends, whole, first


SENDS, WHOLE, FIRST = plan()
STEPS = FIRST + 16


def cdf_and_dens(v):
    e = jnp.exp(v * v * -0.5)
    t = 1.0 / (1.0 + jnp.abs(v) * (0.3275911 * 0.7071067811865476))
    poly = t * (
        0.5 * 0.254829592
        + t
        * (
            0.5 * -0.284496736
            + t * (0.5 * 1.421413741 + t * (0.5 * -1.453152027 + t * (0.5 * 1.061405429)))
        )
    )
    tail = poly * e
    return jnp.where(v > 0, 1.0 - tail, tail), e


def dot(a, b):
    return lax.dot_general(a, b, (((1,), (0,)), ((), ())), preferred_element_type=F32)


def dot_t(a, b):
    return lax.dot_general(a, b, (((1,), (1,)), ((), ())), preferred_element_type=F32)


def fused_kernel(
    klass_ref, off_ref, count_ref, feat_ref, fpn_ref, cot_ref, head_ref, deconv_ref, mask_ref,
    gin_ref, gw_ref,
    wbuf, pyr, frame, fpx, fpt, xs, dpad, hidden, slope, lower, dpre, grad, grad16,
    cols, rows_in, cols_in, corners_in,
    part, acc, core_in, send_a, in_a, acc_b, send_b, in_b, in_c, fin,
    own_sem, send_sem, recv_sem, sib_send, sib_recv, halo_send, halo_recv,
    core_send, core_recv, ring_send, ring_recv,
):
    t = lax.axis_index("tile")
    h = lax.axis_index("head")
    z, x = h // 4, h % 4
    y, core = t // 2, t % 2
    sibling = (t + 1 - 2 * core, h)
    there = (
        (t, z * 4 + (x + 1) % 4),
        (t, z * 4 + (x + 3) % 4),
        (t, (z + 1) % 4 * 4 + x),
        (t, (z + 3) % 4 * 4 + x),
    )
    up, down = (t + 7) % 8, (t + 1) % 8
    left, right = (h + 15) % 16, (h + 1) % 16
    coords = {"x": x, "y": y, "z": z}

    def peer(axis, c):
        if axis == "x":
            return (t, z * 4 + c)
        if axis == "z":
            return (t, c * 4 + x)
        return (c * 2 + core, h)

    base = pl.multiple_of(core * HALF, 16)
    other = pl.multiple_of((1 - core) * HALF, 16)

    own = (
        pltpu.make_async_copy(head_ref, wbuf.at[0, pl.ds(0, 2304)], own_sem.at[0]),
        pltpu.make_async_copy(deconv_ref, wbuf.at[0, pl.ds(2304, 1024)], own_sem.at[1]),
        pltpu.make_async_copy(mask_ref, wbuf.at[0, pl.ds(3328, 32)], own_sem.at[2]),
    )
    for c in own:
        c.start()
    barrier = pltpu.get_barrier_semaphore()
    greeted = [sibling, (up, h), (down, h), (t, left), (t, right)]
    greeted += [(a, b) for a in (up, down) for b in (left, right)]
    for axis in "xyz":
        greeted += [peer(axis, (coords[axis] + d) % 4) for d in (1, 2, 3)]
    for d in greeted:
        pl.semaphore_signal(barrier, inc=1, device_id=d, device_id_type=MESH)

    def piece(n, step):
        d, q, src, dst = SENDS[step][n]
        start, size = PIECES[q]
        rows = pl.ds(pl.multiple_of(base + start, 16), size)
        return pltpu.make_async_remote_copy(
            src_ref=wbuf.at[src, rows],
            dst_ref=wbuf.at[dst, rows],
            send_sem=send_sem.at[d, step],
            recv_sem=recv_sem.at[d, step],
            device_id=there[d],
            device_id_type=MESH,
        )

    def share(slot, mine):
        rows = pl.ds(base if mine else other, HALF)
        return pltpu.make_async_remote_copy(
            src_ref=wbuf.at[slot, rows],
            dst_ref=wbuf.at[slot, rows],
            send_sem=sib_send.at[slot],
            recv_sem=sib_recv.at[slot],
            device_id=sibling,
            device_id_type=MESH,
        )

    def traffic(step):
        if 0 <= step - LAG < len(SENDS):
            for n in range(len(SENDS[step - LAG])):
                piece(n, step - LAG).wait_recv()
        if step < len(SENDS):
            for n in range(len(SENDS[step])):
                piece(n, step).start()
        for slot in range(1, 16):
            if WHOLE[slot] == step:
                share(slot, True).start()
        for slot in range(1, 16):
            if WHOLE[slot] + 1 == step:
                share(slot, False).wait_recv()

    def halo(k, src):
        sides = (
            (src.at[0], rows_in.at[k, 1], (up, h)),
            (src.at[31], rows_in.at[k, 0], (down, h)),
            (cols.at[k, 0], cols_in.at[k, 1], (t, left)),
            (cols.at[k, 1], cols_in.at[k, 0], (t, right)),
            (src.at[0, pl.ds(0, 16)], corners_in.at[k, 3], (up, left)),
            (src.at[0, pl.ds(16, 16)], corners_in.at[k, 2], (up, right)),
            (src.at[31, pl.ds(0, 16)], corners_in.at[k, 1], (down, left)),
            (src.at[31, pl.ds(16, 16)], corners_in.at[k, 0], (down, right)),
        )
        return [
            pltpu.make_async_remote_copy(
                src_ref=a,
                dst_ref=b,
                send_sem=halo_send.at[k, n],
                recv_sem=halo_recv.at[k, n],
                device_id=d,
                device_id_type=MESH,
            )
            for n, (a, b, d) in enumerate(sides)
        ]

    def place_tile(k, values):
        frame[1:33, 8:40, :] = values
        cols[k, 0] = values[:, 0, :].astype(BF16)
        cols[k, 1] = values[:, 31, :].astype(BF16)

    def place_halo(k):
        rows = [rows_in[k, n].astype(F32) for n in range(2)]
        sides = [cols_in[k, n].astype(F32) for n in range(2)]
        corners = [corners_in[k, n].astype(F32) for n in range(4)]
        frame[0, 8:40, :] = jnp.where(t > 0, rows[0], 0.0)
        frame[33, 8:40, :] = jnp.where(t < 7, rows[1], 0.0)
        frame[1:33, 7:8, :] = jnp.where(h > 0, sides[0], 0.0).reshape(32, 1, C)
        frame[1:33, 40:41, :] = jnp.where(h < 15, sides[1], 0.0).reshape(32, 1, C)
        frame[0, 7:8, :] = jnp.where((t > 0) & (h > 0), corners[0][15:16], 0.0)
        frame[0, 40:41, :] = jnp.where((t > 0) & (h < 15), corners[1][0:1], 0.0)
        frame[33, 7:8, :] = jnp.where((t < 7) & (h > 0), corners[2][15:16], 0.0)
        frame[33, 40:41, :] = jnp.where((t < 7) & (h < 15), corners[3][0:1], 0.0)
        for e in range(3):
            fpx[:, e * C : (e + 1) * C] = frame[:, 7 + e : 39 + e, :].reshape(1088, C).astype(BF16)

    place_tile(0, feat_ref[...].astype(F32))
    pl.semaphore_wait(barrier, len(greeted))
    halos = halo(0, feat_ref)
    for c in halos:
        c.start()
    for c in own:
        c.wait()
    traffic(0)
    traffic(1)
    xs[...] = jnp.zeros_like(xs)
    dpad[...] = jnp.zeros_like(dpad)
    grad[...] = jnp.zeros_like(grad)
    for c in halos:
        c.wait_recv()
    place_halo(0)
    traffic(2)
    for m in range(4):
        value = jnp.zeros((256, C), F32)
        for a in range(3):
            taps = fpx[a * 32 + m * 256 : a * 32 + (m + 1) * 256, :]
            value += dot(taps, fpn_ref[a * 3 * C : (a + 1) * 3 * C, :])
        pyr[m * 256 : (m + 1) * 256, :] = value.astype(BF16)
    traffic(3)
    for a in range(3):
        for e in range(3):
            fpt[(a * 3 + e) * C : (a * 3 + e + 1) * C, :] = jnp.transpose(
                fpx[a * 32 : a * 32 + 1024, e * C : (e + 1) * C]
            )
    traffic(4)

    def widen():
        for e in range(3):
            xs[:, 16:240, e * C : (e + 1) * C] = dpad[:, 15 + e : 239 + e, :].astype(BF16)

    def compute(p):
        dz = jnp.int32(0)
        dx = jnp.int32(0)
        for k in range(1, 16):
            dz = jnp.where(p == k, SLOTS[k][0], dz)
            dx = jnp.where(p == k, SLOTS[k][1], dx)
        klass = (z + 4 - dz) % 4 * 4 + (x + 4 - dx) % 4
        count = count_ref[0]
        slots = [jnp.int32(-1), jnp.int32(-1)]
        bases = [jnp.int32(-1), jnp.int32(-1)]
        for s in range(16):
            hit = (klass_ref[s] == klass) & (s < count)
            corner = off_ref[2 * s] * 32 + off_ref[2 * s + 1]
            again = hit & (slots[0] >= 0)
            only = hit & (slots[0] < 0)
            slots = [jnp.where(only, s, slots[0]), jnp.where(again, s, slots[1])]
            bases = [jnp.where(only, corner, bases[0]), jnp.where(again, corner, bases[1])]

        def places(axis):
            r = lax.broadcasted_iota(jnp.int32, (224, 1) if axis == 0 else (1, 224), axis)
            i, j = r // 16, r % 16
            spots = [jnp.where((j < 14) & (b >= 0), b + i * 32 + j, -1) for b in bases]
            return jnp.concatenate(spots, axis=axis)

        pixel = lax.broadcasted_iota(jnp.int32, (448, 1024), 1)
        pick = jnp.where(pixel == places(0), 1.0, 0.0).astype(BF16)
        dpad[:, 16:240, :] = dot(pick, pyr[...]).reshape(2, 224, C)
        widen()
        pre_one = jnp.zeros((448, C), F32)
        for a in range(3):
            taps = xs[:, a * 16 : a * 16 + 224, :].reshape(448, 3 * C)
            pre_one += dot(taps, wbuf[p, a * 3 * C : (a + 1) * 3 * C, :])
        phi, e = cdf_and_dens(pre_one)
        hidden[...] = (pre_one * phi).astype(BF16)
        slope[...] = phi + pre_one * e * 0.3989422804014327
        gain = wbuf[p, 3328:3344, :][0:1].astype(F32)
        line = lax.broadcasted_iota(jnp.int32, (128, C), 0) % 64
        for q in range(4):
            kernel = wbuf[p, 2304 + q * C : 2304 + (q + 1) * C, :]
            for b in range(2):
                rows = slice(b * 224, (b + 1) * 224)
                chosen = jnp.where((line == 4 * slots[b] + q) & (slots[b] >= 0), gain, 0.0)
                upper = dot(cot_ref[...], chosen.astype(BF16))
                pre_two = dot(hidden[rows, :], kernel)
                phi, e = cdf_and_dens(pre_two)
                dpre[rows, :] = (upper * (phi + pre_two * e * 0.3989422804014327)).astype(BF16)
                part_low = dot_t(dpre[rows, :], kernel)
                if q == 0:
                    lower[rows, :] = part_low
                else:
                    lower[rows, :] += part_low
        dpad[:, 16:240, :] = (lower[...] * slope[...]).reshape(2, 224, C)
        widen()
        total = jnp.zeros((448, C), F32)
        for a in range(3):
            for e in range(3):
                taps = xs[:, a * 16 : a * 16 + 224, e * C : (e + 1) * C].reshape(448, C)
                tap = (2 - a) * 3 + 2 - e
                total += dot_t(taps, wbuf[p, tap * C : (tap + 1) * C, :])
        pixel = lax.broadcasted_iota(jnp.int32, (1024, 448), 0)
        spread = jnp.where(pixel == places(1), 1.0, 0.0).astype(BF16)
        grad[...] += dot(spread, total.astype(BF16))

    def step_body(step, carry):
        for s in range(FIRST, len(SENDS) + LAG + 2):
            pl.when(step == s)(functools.partial(traffic, s))
        compute(step - FIRST)
        return carry

    lax.fori_loop(FIRST, STEPS, step_body, 0)

    rounded = grad[...].astype(BF16)
    grad16[...] = rounded.reshape(32, 32, C)
    place_tile(1, grad16[...].astype(F32))
    halos_grad = halo(1, grad16)
    for c in halos_grad:
        c.start()
    for m in range(9):
        value = dot(fpt[m * C : (m + 1) * C, :], grad16[...].reshape(1024, C))
        rows = slice(m * C, (m + 1) * C)
        part[0, rows, :] = value[:, :128].astype(BF16)
        part[1, rows, :] = value[:, 128:].astype(BF16)
        acc[rows, :] = jnp.where(core == 0, value[:, :128], value[:, 128:])
    swap = pltpu.make_async_remote_copy(
        src_ref=part.at[1 - core],
        dst_ref=core_in,
        send_sem=core_send.at[0],
        recv_sem=core_recv.at[0],
        device_id=sibling,
        device_id_type=MESH,
    )
    swap.start()

    for c in halos_grad:
        c.wait_recv()
    place_halo(1)
    for m in range(4):
        value = jnp.zeros((256, C), F32)
        for a in range(3):
            for e in range(3):
                taps = fpx[a * 32 + m * 256 : a * 32 + (m + 1) * 256, e * C : (e + 1) * C]
                tap = (2 - a) * 3 + 2 - e
                value += dot_t(taps, fpn_ref[tap * C : (tap + 1) * C, :])
        gin_ref[m * 256 : (m + 1) * 256, :] = value.astype(BF16)

    def ring(phase, g, d, axis, src, dst):
        return pltpu.make_async_remote_copy(
            src_ref=src,
            dst_ref=dst,
            send_sem=ring_send.at[phase, g, d - 1],
            recv_sem=ring_recv.at[phase, g, d - 1],
            device_id=peer(axis, (coords[axis] + d) % 4),
            device_id_type=MESH,
        )

    def span(start, size):
        return pl.ds(pl.multiple_of(start, 16), size)

    orders = ("yxz", "xzy", "zyx")
    groups = [(g, *[coords[a] for a in orders[g]]) for g in range(3)]

    swap.wait()
    for m in range(9):
        rows = slice(m * C, (m + 1) * C)
        value = acc[rows, :] + core_in[rows, :].astype(F32)
        acc[rows, :] = value
        send_a[rows, :] = value.astype(BF16)

    def out_a(g, ca, d):
        return ring(
            0, g, d, orders[g][0],
            send_a.at[span(768 * g + 192 * ((ca + d) % 4), 192)],
            in_a.at[g, ca],
        )

    def out_b(g, cb, d):
        return ring(1, g, d, orders[g][1], send_b.at[g, span(48 * ((cb + d) % 4), 48)], in_b.at[g, cb])

    def out_c(g, cc, d):
        return ring(2, g, d, orders[g][2], in_c.at[g, cc], in_c.at[g, cc])

    def back_b(g, ca, cb, d):
        rows = span(768 * g + 192 * ca + 48 * cb, 48)
        return ring(3, g, d, orders[g][1], fin.at[core, rows], fin.at[core, rows])

    def back_a(g, ca, d):
        rows = span(768 * g + 192 * ca, 192)
        return ring(4, g, d, orders[g][0], fin.at[core, rows], fin.at[core, rows])

    far = (1, 2, 3)
    for g, ca, cb, cc in groups:
        for d in far:
            out_a(g, ca, d).start()
    for g, ca, cb, cc in groups:
        value = acc[span(768 * g + 192 * ca, 192), :]
        for d in far:
            out_a(g, (ca + 4 - d) % 4, d).wait_recv()
            value += in_a[g, (ca + 4 - d) % 4].astype(F32)
        acc_b[g] = value
        send_b[g] = value.astype(BF16)
        for d in far:
            out_b(g, cb, d).start()
    for g, ca, cb, cc in groups:
        value = acc_b[g, span(48 * cb, 48), :]
        for d in far:
            out_b(g, (cb + 4 - d) % 4, d).wait_recv()
            value += in_b[g, (cb + 4 - d) % 4].astype(F32)
        in_c[g, cc] = value.astype(BF16)
        for d in far:
            out_c(g, cc, d).start()
    for g, ca, cb, cc in groups:
        for d in far:
            out_c(g, (cc + 4 - d) % 4, d).wait_recv()
        value = in_c[g, 0].astype(F32)
        for n in far:
            value += in_c[g, n].astype(F32)
        fin[core, span(768 * g + 192 * ca + 48 * cb, 48), :] = value.astype(BF16)
        for d in far:
            back_b(g, ca, cb, d).start()
    for g, ca, cb, cc in groups:
        for d in far:
            back_b(g, ca, (cb + 4 - d) % 4, d).wait_recv()
        for d in far:
            back_a(g, ca, d).start()
    for g, ca, cb, cc in groups:
        for d in far:
            back_a(g, (ca + 4 - d) % 4, d).wait_recv()

    def mirror(mine):
        half = fin.at[core if mine else 1 - core]
        return pltpu.make_async_remote_copy(
            src_ref=half,
            dst_ref=half,
            send_sem=core_send.at[1],
            recv_sem=core_recv.at[1],
            device_id=sibling,
            device_id_type=MESH,
        )

    mirror(True).start()
    for step in range(len(SENDS)):
        for n in range(len(SENDS[step])):
            piece(n, step).wait_send()
    for slot in range(1, 16):
        share(slot, True).wait_send()
    for c in (*halos, *halos_grad):
        c.wait_send()
    for g, ca, cb, cc in groups:
        for d in far:
            out_a(g, ca, d).wait_send()
            out_b(g, cb, d).wait_send()
            out_c(g, cc, d).wait_send()
            back_b(g, ca, cb, d).wait_send()
            back_a(g, ca, d).wait_send()
    mirror(True).wait_send()
    mirror(False).wait_recv()
    gw_ref[:, :128] = fin[0].astype(F32) * (1.0 / TOTAL)
    gw_ref[:, 128:] = fin[1].astype(F32) * (1.0 / TOTAL)


def local(
    feature_map,
    fpn_weight,
    head_weight,
    deconv_weight,
    mask_weight,
    box_class,
    box_offset,
    valid_count,
    mask_cotangent,
):
    cot = mask_cotangent.reshape(16, 14, 2, 14, 2).transpose(1, 3, 0, 2, 4).reshape(14, 14, 64)
    cot = jnp.pad(cot, ((0, 0), (0, 2), (0, 0))).reshape(224, 64)
    high = cot.astype(BF16)
    cot = jnp.concatenate([high, (cot - high.astype(F32)).astype(BF16)], axis=1)
    mask = jnp.pad(jnp.broadcast_to(mask_weight, (16, C)), ((0, 16), (0, 0)))
    smem = pl.BlockSpec(memory_space=pltpu.SMEM)
    vmem = pl.BlockSpec(memory_space=pltpu.VMEM)
    hbm = pl.BlockSpec(memory_space=pl.ANY)
    sends = len(SENDS)
    dma = pltpu.SemaphoreType.DMA
    grad_input, grad_weight = pl.pallas_call(
        fused_kernel,
        out_shape=(
            jax.ShapeDtypeStruct((1024, C), BF16),
            jax.ShapeDtypeStruct((2304, C), F32),
        ),
        in_specs=[smem, smem, smem, vmem, vmem, vmem, hbm, hbm, hbm],
        out_specs=(vmem, vmem),
        scratch_shapes=[
            pltpu.VMEM((16, ROWS, C), BF16),
            pltpu.VMEM((1024, C), BF16),
            pltpu.VMEM((34, 48, C), F32),
            pltpu.VMEM((1088, 3 * C), BF16),
            pltpu.VMEM((2304, 1024), BF16),
            pltpu.VMEM((2, 256, 3 * C), BF16),
            pltpu.VMEM((2, 256, C), F32),
            pltpu.VMEM((448, C), BF16),
            pltpu.VMEM((448, C), F32),
            pltpu.VMEM((448, C), F32),
            pltpu.VMEM((448, C), BF16),
            pltpu.VMEM((1024, C), F32),
            pltpu.VMEM((32, 32, C), BF16),
            pltpu.VMEM((2, 2, 32, C), BF16),
            pltpu.VMEM((2, 2, 32, C), BF16),
            pltpu.VMEM((2, 2, 32, C), BF16),
            pltpu.VMEM((2, 4, 16, C), BF16),
            pltpu.VMEM((2, 2304, 128), BF16),
            pltpu.VMEM((2304, 128), F32),
            pltpu.VMEM((2304, 128), BF16),
            pltpu.VMEM((2304, 128), BF16),
            pltpu.VMEM((3, 4, 192, 128), BF16),
            pltpu.VMEM((3, 192, 128), F32),
            pltpu.VMEM((3, 192, 128), BF16),
            pltpu.VMEM((3, 4, 48, 128), BF16),
            pltpu.VMEM((3, 4, 48, 128), BF16),
            pltpu.VMEM((2, 2304, 128), BF16),
            dma((3,)),
            dma((4, sends)),
            dma((4, sends)),
            dma((16,)),
            dma((16,)),
            dma((2, 8)),
            dma((2, 8)),
            dma((2,)),
            dma((2,)),
            dma((5, 3, 3)),
            dma((5, 3, 3)),
        ],
        compiler_params=pltpu.CompilerParams(
            collective_id=0, has_side_effects=True, vmem_limit_bytes=60 * 1024 * 1024
        ),
    )(
        box_class,
        box_offset.reshape(32),
        valid_count,
        feature_map,
        fpn_weight.reshape(2304, C),
        cot,
        head_weight.reshape(2304, C),
        deconv_weight.reshape(1024, C),
        mask,
    )
    return grad_input.reshape(32, 32, C), grad_weight.reshape(3, 3, C, C)


def solution(mesh):
    in_specs = (
        P("tile", "head", None),
        P(),
        P("head", None, None, None, None),
        P("head", None, None, None, None),
        P("head", None),
        P(("tile", "head")),
        P(("tile", "head"), None),
        P(("tile", "head")),
        P(("tile", "head"), None, None),
    )
    out_specs = (P("tile", "head", None), P())
    return jax.shard_map(local, mesh=mesh, in_specs=in_specs, out_specs=out_specs, check_vma=False)
```

```python
import functools

import jax
import jax.numpy as jnp
from jax import lax
from jax.experimental import pallas as pl
from jax.experimental.pallas import tpu as pltpu
from jax.sharding import PartitionSpec as P

MESH = pl.DeviceIdType.MESH
F32 = jnp.float32
BF16 = jnp.bfloat16

C = 256
HALF = 1680
ROWS = 2 * HALF
PIECES = ((0, 416), (416, 416), (832, 416), (1248, 432))
LAG = 2
PACE = 0.95
SLOTS = (
    (0, 0), (3, 0), (1, 0), (1, 3), (3, 1), (0, 1), (0, 3), (1, 1),
    (3, 3), (0, 2), (2, 0), (3, 2), (2, 3), (1, 2), (2, 1), (2, 2),
)
DIRS = ("x+", "x-", "z+", "z-")
TOTAL = 2048


def plan():
    def hop(d, plus):
        if d == 1:
            return 0, "+"
        if d == 3:
            return 0, "-"
        return (1, "+") if plus else (3, "-")

    left = {d: [] for d in DIRS}
    for q in range(4):
        plus = q % 2 == 0
        for slot in SLOTS[1:]:
            dz, dx = slot
            if (dz if q < 2 else not dx):
                before, sign = hop(dz, plus)
                left["z" + sign].append((q, (before, dx), slot))
            else:
                before, sign = hop(dx, plus)
                left["x" + sign].append((q, (dz, before), slot))
    rank = {s: i for i, s in enumerate(SLOTS)}
    ready = {(q, (0, 0)): 0 for q in range(4)}
    sends = []
    while any(left.values()):
        step = len(sends)
        now = []
        for d in DIRS:
            can = [e for e in left[d] if ready.get((e[0], e[1]), 99) <= step]
            if can:
                e = min(can, key=lambda e: rank[e[2]])
                left[d].remove(e)
                ready[(e[0], e[2])] = step + LAG
                now.append((DIRS.index(d), e[0], rank[e[1]], rank[e[2]]))
        sends.append(now)
    whole = [0] + [max(ready[(q, s)] for q in range(4)) for s in SLOTS[1:]]
    order = sorted(range(16), key=lambda i: whole[i])
    new = {old: i for i, old in enumerate(order)}
    sends = [[(d, q, new[a], new[b]) for d, q, a, b in now] for now in sends]
    return sends, [whole[i] for i in order], [SLOTS[i] for i in order]


SENDS, WHOLE, SLOTS = plan()
EARLY = 4
ENDS = [EARLY] + [max(WHOLE[p] + 1, int(6 + PACE * (p - 1))) for p in range(1, 16)]
ENDS = [min(e, len(SENDS) + LAG + 1) for e in ENDS]


def cdf_and_dens(v):
    e = jnp.exp2(v * v * (-0.5 * 1.4426950408889634))
    d = 1.0 + jnp.abs(v) * (0.3275911 * 0.7071067811865476)
    t = pl.reciprocal(d, approx=True)
    t = t * (2.0 - d * t)
    poly = t * (
        0.5 * 0.254829592
        + t
        * (
            0.5 * -0.284496736
            + t * (0.5 * 1.421413741 + t * (0.5 * -1.453152027 + t * (0.5 * 1.061405429)))
        )
    )
    tail = poly * e
    return jnp.where(v > 0, 1.0 - tail, tail), e


def dot(a, b):
    return lax.dot_general(a, b, (((1,), (0,)), ((), ())), preferred_element_type=F32)


def dot_t(a, b):
    return lax.dot_general(a, b, (((1,), (1,)), ((), ())), preferred_element_type=F32)


def fused_kernel(
    klass_ref, off_ref, count_ref, feat_ref, fpn_ref, cot_ref, head_ref, deconv_ref, mask_ref,
    gin_ref, gw_ref,
    wbuf, pyr, frame, fpx, fpt, xs, hidden, slope, total, dpre, grad, grad16,
    cols, rows_in, cols_in, corners_in,
    part, acc, core_in, send_a, in_a, acc_b, send_b, in_b, in_c, fin,
    own_sem, send_sem, recv_sem, sib_send, sib_recv, halo_send, halo_recv,
    core_send, core_recv, ring_send, ring_recv,
):
    t = lax.axis_index("tile")
    h = lax.axis_index("head")
    z, x = h // 4, h % 4
    y, core = t // 2, t % 2
    sibling = (t + 1 - 2 * core, h)
    there = (
        (t, z * 4 + (x + 1) % 4),
        (t, z * 4 + (x + 3) % 4),
        (t, (z + 1) % 4 * 4 + x),
        (t, (z + 3) % 4 * 4 + x),
    )
    up, down = (t + 7) % 8, (t + 1) % 8
    left, right = (h + 15) % 16, (h + 1) % 16
    coords = {"x": x, "y": y, "z": z}

    def peer(axis, c):
        if axis == "x":
            return (t, z * 4 + c)
        if axis == "z":
            return (t, c * 4 + x)
        return (c * 2 + core, h)

    base = pl.multiple_of(core * HALF, 16)
    other = pl.multiple_of((1 - core) * HALF, 16)

    own = (
        pltpu.make_async_copy(head_ref, wbuf.at[0, pl.ds(0, 2304)], own_sem.at[0]),
        pltpu.make_async_copy(deconv_ref, wbuf.at[0, pl.ds(2304, 1024)], own_sem.at[1]),
    )
    for c in own:
        c.start()
    barrier = pltpu.get_barrier_semaphore()
    greeted = [sibling, (up, h), (down, h), (t, left), (t, right)]
    greeted += [(a, b) for a in (up, down) for b in (left, right)]
    for axis in "xyz":
        greeted += [peer(axis, (coords[axis] + d) % 4) for d in (1, 2, 3)]
    for d in greeted:
        pl.semaphore_signal(barrier, inc=1, device_id=d, device_id_type=MESH)

    def piece(n, step):
        d, q, src, dst = SENDS[step][n]
        start, size = PIECES[q]
        rows = pl.ds(pl.multiple_of(base + start, 16), size)
        return pltpu.make_async_remote_copy(
            src_ref=wbuf.at[src, rows],
            dst_ref=wbuf.at[dst, rows],
            send_sem=send_sem.at[d, step],
            recv_sem=recv_sem.at[d, step],
            device_id=there[d],
            device_id_type=MESH,
        )

    def share(slot, mine):
        rows = pl.ds(base if mine else other, HALF)
        return pltpu.make_async_remote_copy(
            src_ref=wbuf.at[slot, rows],
            dst_ref=wbuf.at[slot, rows],
            send_sem=sib_send.at[slot],
            recv_sem=sib_recv.at[slot],
            device_id=sibling,
            device_id_type=MESH,
        )

    def traffic(step):
        if 0 <= step - LAG < len(SENDS):
            for n in range(len(SENDS[step - LAG])):
                piece(n, step - LAG).wait_recv()
        if step < len(SENDS):
            for n in range(len(SENDS[step])):
                piece(n, step).start()
        for slot in range(1, 16):
            if WHOLE[slot] == step:
                share(slot, True).start()
        for slot in range(1, 16):
            if WHOLE[slot] + 1 == step:
                share(slot, False).wait_recv()

    def halo(k, src):
        sides = (
            (src.at[0], rows_in.at[k, 1], (up, h)),
            (src.at[31], rows_in.at[k, 0], (down, h)),
            (cols.at[k, 0], cols_in.at[k, 1], (t, left)),
            (cols.at[k, 1], cols_in.at[k, 0], (t, right)),
            (src.at[0, pl.ds(0, 16)], corners_in.at[k, 3], (up, left)),
            (src.at[0, pl.ds(16, 16)], corners_in.at[k, 2], (up, right)),
            (src.at[31, pl.ds(0, 16)], corners_in.at[k, 1], (down, left)),
            (src.at[31, pl.ds(16, 16)], corners_in.at[k, 0], (down, right)),
        )
        return [
            pltpu.make_async_remote_copy(
                src_ref=a,
                dst_ref=b,
                send_sem=halo_send.at[k, n],
                recv_sem=halo_recv.at[k, n],
                device_id=d,
                device_id_type=MESH,
            )
            for n, (a, b, d) in enumerate(sides)
        ]

    def place_tile(k, values):
        frame[1:33, 8:40, :] = values
        cols[k, 0] = values[:, 0, :].astype(BF16)
        cols[k, 1] = values[:, 31, :].astype(BF16)

    def place_halo(k):
        rows = [rows_in[k, n].astype(F32) for n in range(2)]
        sides = [cols_in[k, n].astype(F32) for n in range(2)]
        corners = [corners_in[k, n].astype(F32) for n in range(4)]
        frame[0, 8:40, :] = jnp.where(t > 0, rows[0], 0.0)
        frame[33, 8:40, :] = jnp.where(t < 7, rows[1], 0.0)
        frame[1:33, 7:8, :] = jnp.where(h > 0, sides[0], 0.0).reshape(32, 1, C)
        frame[1:33, 40:41, :] = jnp.where(h < 15, sides[1], 0.0).reshape(32, 1, C)
        frame[0, 7:8, :] = jnp.where((t > 0) & (h > 0), corners[0][15:16], 0.0)
        frame[0, 40:41, :] = jnp.where((t > 0) & (h < 15), corners[1][0:1], 0.0)
        frame[33, 7:8, :] = jnp.where((t < 7) & (h > 0), corners[2][15:16], 0.0)
        frame[33, 40:41, :] = jnp.where((t < 7) & (h < 15), corners[3][0:1], 0.0)
        for e in range(3):
            fpx[:, e * C : (e + 1) * C] = frame[:, 7 + e : 39 + e, :].reshape(1088, C).astype(BF16)

    place_tile(0, feat_ref[...].astype(F32))
    pl.semaphore_wait(barrier, len(greeted))
    halos = halo(0, feat_ref)
    for c in halos:
        c.start()
    wbuf[0, 3328:3360, :] = jnp.broadcast_to(mask_ref[...].astype(F32), (32, C)).astype(BF16)
    for c in own:
        c.wait()
    traffic(0)
    traffic(1)
    xs[...] = jnp.zeros_like(xs)
    grad[...] = jnp.zeros_like(grad)
    for c in halos:
        c.wait_recv()
    place_halo(0)
    traffic(2)
    for m in range(4):
        value = jnp.zeros((256, C), F32)
        for a in range(3):
            taps = fpx[a * 32 + m * 256 : a * 32 + (m + 1) * 256, :]
            value += dot(taps, fpn_ref[a * 3 * C : (a + 1) * 3 * C, :])
        pyr[m * 256 : (m + 1) * 256, :] = value.astype(BF16)
    traffic(3)
    for a in range(3):
        for e in range(3):
            fpt[(a * 3 + e) * C : (a * 3 + e + 1) * C, :] = jnp.transpose(
                fpx[a * 32 : a * 32 + 1024, e * C : (e + 1) * C]
            )

    def widen(b, value):
        xs[b, 16:240, C : 2 * C] = value.astype(BF16)
        xs[b, 16:240, 0:C] = pltpu.roll(value, 1, 0).astype(BF16)
        xs[b, 16:240, 2 * C :] = pltpu.roll(value, 223, 0).astype(BF16)

    def compute(p):
        dz = jnp.int32(0)
        dx = jnp.int32(0)
        for k in range(1, 16):
            dz = jnp.where(p == k, SLOTS[k][0], dz)
            dx = jnp.where(p == k, SLOTS[k][1], dx)
        klass = (z + 4 - dz) % 4 * 4 + (x + 4 - dx) % 4
        count = count_ref[0]
        slots = [jnp.int32(-1), jnp.int32(-1)]
        bases = [jnp.int32(-1), jnp.int32(-1)]
        for s in range(16):
            hit = (klass_ref[s] == klass) & (s < count)
            corner = off_ref[2 * s] * 32 + off_ref[2 * s + 1]
            again = hit & (slots[0] >= 0)
            only = hit & (slots[0] < 0)
            slots = [jnp.where(only, s, slots[0]), jnp.where(again, s, slots[1])]
            bases = [jnp.where(only, corner, bases[0]), jnp.where(again, corner, bases[1])]

        def places(axis):
            r = lax.broadcasted_iota(jnp.int32, (224, 1) if axis == 0 else (1, 224), axis)
            i, j = r // 16, r % 16
            spots = [jnp.where((j < 14) & (b >= 0), b + i * 32 + j, -1) for b in bases]
            return jnp.concatenate(spots, axis=axis)

        pixel = lax.broadcasted_iota(jnp.int32, (224, 1024), 1)
        spots = places(0)
        for b in range(2):
            pick = jnp.where(pixel == spots[b * 224 : (b + 1) * 224], 1.0, 0.0).astype(BF16)
            widen(b, dot(pick, pyr[...]))
        for b in range(2):
            rows = slice(b * 224, (b + 1) * 224)
            value = dot(xs[b, 0:224, :], wbuf[p, 0 : 3 * C, :])
            value += dot(xs[b, 16:240, :], wbuf[p, 3 * C : 6 * C, :])
            value += dot(xs[b, 32:256, :], wbuf[p, 6 * C : 9 * C, :])
            pre_one = value
            phi, e = cdf_and_dens(pre_one)
            hidden[rows, :] = (pre_one * phi).astype(BF16)
            slope[rows, :] = phi + pre_one * e * 0.3989422804014327
        gain = wbuf[p, 3328:3344, :][0:1].astype(F32)
        line = lax.broadcasted_iota(jnp.int32, (128, C), 0) % 64
        kernels = [wbuf[p, 2304 + q * C : 2304 + (q + 1) * C, :] for q in range(4)]
        for q in range(4):
            for b in range(2):
                rows = slice(b * 224, (b + 1) * 224)
                chosen = jnp.where((line == 4 * slots[b] + q) & (slots[b] >= 0), gain, 0.0)
                upper = dot(cot_ref[...], chosen.astype(BF16))
                pre_two = dot(hidden[rows, :], kernels[q])
                phi, e = cdf_and_dens(pre_two)
                value = upper * (phi + pre_two * e * 0.3989422804014327)
                dpre[rows, q * C : (q + 1) * C] = value.astype(BF16)
        for b in range(2):
            rows = slice(b * 224, (b + 1) * 224)
            value = dot_t(dpre[rows, 0:C], kernels[0])
            for q in range(1, 4):
                value += dot_t(dpre[rows, q * C : (q + 1) * C], kernels[q])
            widen(b, value * slope[rows, :])
        for b in range(2):
            value = jnp.zeros((224, C), F32)
            for a in range(3):
                for e in range(3):
                    tap = (2 - a) * 3 + 2 - e
                    value += dot_t(
                        xs[b, a * 16 : a * 16 + 224, e * C : (e + 1) * C],
                        wbuf[p, tap * C : (tap + 1) * C, :],
                    )
            total[b * 224 : (b + 1) * 224, :] = value.astype(BF16)
        pixel = lax.broadcasted_iota(jnp.int32, (1024, 448), 0)
        spread = jnp.where(pixel == places(1), 1.0, 0.0).astype(BF16)
        grad[...] += dot(spread, total[...])

    def advance(p):
        for step in range(EARLY if p == 0 else ENDS[p - 1] + 1, ENDS[p] + 1):
            traffic(step)

    def class_body(p, carry):
        for n in range(16):
            pl.when(p == n)(functools.partial(advance, n))
        compute(p)
        return carry

    lax.fori_loop(0, 16, class_body, 0)

    rounded = grad[...].astype(BF16)
    grad16[...] = rounded.reshape(32, 32, C)
    place_tile(1, grad16[...].astype(F32))
    halos_grad = halo(1, grad16)
    for c in halos_grad:
        c.start()
    for m in range(9):
        value = dot(fpt[m * C : (m + 1) * C, :], grad16[...].reshape(1024, C))
        rows = slice(m * C, (m + 1) * C)
        part[0, rows, :] = value[:, :128].astype(BF16)
        part[1, rows, :] = value[:, 128:].astype(BF16)
        acc[rows, :] = jnp.where(core == 0, value[:, :128], value[:, 128:])
    swap = pltpu.make_async_remote_copy(
        src_ref=part.at[1 - core],
        dst_ref=core_in,
        send_sem=core_send.at[0],
        recv_sem=core_recv.at[0],
        device_id=sibling,
        device_id_type=MESH,
    )
    swap.start()

    for c in halos_grad:
        c.wait_recv()
    place_halo(1)

    def back_conv(m):
        value = jnp.zeros((256, C), F32)
        for a in range(3):
            for e in range(3):
                taps = fpx[a * 32 + m * 256 : a * 32 + (m + 1) * 256, e * C : (e + 1) * C]
                tap = (2 - a) * 3 + 2 - e
                value += dot_t(taps, fpn_ref[tap * C : (tap + 1) * C, :])
        gin_ref[m * 256 : (m + 1) * 256, :] = value.astype(BF16)

    def ring(phase, g, d, axis, src, dst):
        return pltpu.make_async_remote_copy(
            src_ref=src,
            dst_ref=dst,
            send_sem=ring_send.at[phase, g, d - 1],
            recv_sem=ring_recv.at[phase, g, d - 1],
            device_id=peer(axis, (coords[axis] + d) % 4),
            device_id_type=MESH,
        )

    def span(start, size):
        return pl.ds(pl.multiple_of(start, 16), size)

    orders = ("yxz", "xzy", "zyx")
    groups = [(g, *[coords[a] for a in orders[g]]) for g in range(3)]

    swap.wait()
    for m in range(9):
        rows = slice(m * C, (m + 1) * C)
        value = acc[rows, :] + core_in[rows, :].astype(F32)
        acc[rows, :] = value
        send_a[rows, :] = value.astype(BF16)

    def out_a(g, ca, d):
        return ring(
            0, g, d, orders[g][0],
            send_a.at[span(768 * g + 192 * ((ca + d) % 4), 192)],
            in_a.at[g, ca],
        )

    def out_b(g, cb, d):
        return ring(1, g, d, orders[g][1], send_b.at[g, span(48 * ((cb + d) % 4), 48)], in_b.at[g, cb])

    def out_c(g, cc, d):
        return ring(2, g, d, orders[g][2], in_c.at[g, cc], in_c.at[g, cc])

    def back_b(g, ca, cb, d):
        rows = span(768 * g + 192 * ca + 48 * cb, 48)
        return ring(3, g, d, orders[g][1], fin.at[core, rows], fin.at[core, rows])

    def back_a(g, ca, d):
        rows = span(768 * g + 192 * ca, 192)
        return ring(4, g, d, orders[g][0], fin.at[core, rows], fin.at[core, rows])

    far = (1, 2, 3)
    for g, ca, cb, cc in groups:
        for d in far:
            out_a(g, ca, d).start()
    back_conv(0)
    for g, ca, cb, cc in groups:
        value = acc[span(768 * g + 192 * ca, 192), :]
        for d in far:
            out_a(g, (ca + 4 - d) % 4, d).wait_recv()
            value += in_a[g, (ca + 4 - d) % 4].astype(F32)
        acc_b[g] = value
        send_b[g] = value.astype(BF16)
        for d in far:
            out_b(g, cb, d).start()
    back_conv(1)
    for g, ca, cb, cc in groups:
        value = acc_b[g, span(48 * cb, 48), :]
        for d in far:
            out_b(g, (cb + 4 - d) % 4, d).wait_recv()
            value += in_b[g, (cb + 4 - d) % 4].astype(F32)
        in_c[g, cc] = value.astype(BF16)
        for d in far:
            out_c(g, cc, d).start()
    back_conv(2)
    for g, ca, cb, cc in groups:
        for d in far:
            out_c(g, (cc + 4 - d) % 4, d).wait_recv()
        value = in_c[g, 0].astype(F32)
        for n in far:
            value += in_c[g, n].astype(F32)
        fin[core, span(768 * g + 192 * ca + 48 * cb, 48), :] = value.astype(BF16)
        for d in far:
            back_b(g, ca, cb, d).start()
    back_conv(3)
    for g, ca, cb, cc in groups:
        for d in far:
            back_b(g, ca, (cb + 4 - d) % 4, d).wait_recv()
        for d in far:
            back_a(g, ca, d).start()
    for g, ca, cb, cc in groups:
        for d in far:
            back_a(g, (ca + 4 - d) % 4, d).wait_recv()

    def mirror(mine):
        half = fin.at[core if mine else 1 - core]
        return pltpu.make_async_remote_copy(
            src_ref=half,
            dst_ref=half,
            send_sem=core_send.at[1],
            recv_sem=core_recv.at[1],
            device_id=sibling,
            device_id_type=MESH,
        )

    mirror(True).start()
    for step in range(len(SENDS)):
        for n in range(len(SENDS[step])):
            piece(n, step).wait_send()
    for slot in range(1, 16):
        share(slot, True).wait_send()
    for c in (*halos, *halos_grad):
        c.wait_send()
    for g, ca, cb, cc in groups:
        for d in far:
            out_a(g, ca, d).wait_send()
            out_b(g, cb, d).wait_send()
            out_c(g, cc, d).wait_send()
            back_b(g, ca, cb, d).wait_send()
            back_a(g, ca, d).wait_send()
    mirror(True).wait_send()
    mirror(False).wait_recv()
    gw_ref[:, :128] = fin[0]
    gw_ref[:, 128:] = fin[1]


def local(
    feature_map,
    fpn_weight,
    head_weight,
    deconv_weight,
    mask_weight,
    box_class,
    box_offset,
    valid_count,
    mask_cotangent,
):
    cot = mask_cotangent.reshape(16, 14, 2, 14, 2).transpose(1, 3, 0, 2, 4).reshape(14, 14, 64)
    cot = jnp.pad(cot, ((0, 0), (0, 2), (0, 0))).reshape(224, 64)
    high = cot.astype(BF16)
    cot = jnp.concatenate([high, (cot - high.astype(F32)).astype(BF16)], axis=1)
    smem = pl.BlockSpec(memory_space=pltpu.SMEM)
    vmem = pl.BlockSpec(memory_space=pltpu.VMEM)
    hbm = pl.BlockSpec(memory_space=pl.ANY)
    sends = len(SENDS)
    dma = pltpu.SemaphoreType.DMA
    grad_input, grad_weight = pl.pallas_call(
        fused_kernel,
        out_shape=(
            jax.ShapeDtypeStruct((1024, C), BF16),
            jax.ShapeDtypeStruct((2304, C), BF16),
        ),
        in_specs=[smem, smem, smem, vmem, vmem, vmem, hbm, hbm, vmem],
        out_specs=(vmem, vmem),
        scratch_shapes=[
            pltpu.VMEM((16, ROWS, C), BF16),
            pltpu.VMEM((1024, C), BF16),
            pltpu.VMEM((34, 48, C), F32),
            pltpu.VMEM((1088, 3 * C), BF16),
            pltpu.VMEM((2304, 1024), BF16),
            pltpu.VMEM((2, 256, 3 * C), BF16),
            pltpu.VMEM((448, C), BF16),
            pltpu.VMEM((448, C), F32),
            pltpu.VMEM((448, C), BF16),
            pltpu.VMEM((448, 4 * C), BF16),
            pltpu.VMEM((1024, C), F32),
            pltpu.VMEM((32, 32, C), BF16),
            pltpu.VMEM((2, 2, 32, C), BF16),
            pltpu.VMEM((2, 2, 32, C), BF16),
            pltpu.VMEM((2, 2, 32, C), BF16),
            pltpu.VMEM((2, 4, 16, C), BF16),
            pltpu.VMEM((2, 2304, 128), BF16),
            pltpu.VMEM((2304, 128), F32),
            pltpu.VMEM((2304, 128), BF16),
            pltpu.VMEM((2304, 128), BF16),
            pltpu.VMEM((3, 4, 192, 128), BF16),
            pltpu.VMEM((3, 192, 128), F32),
            pltpu.VMEM((3, 192, 128), BF16),
            pltpu.VMEM((3, 4, 48, 128), BF16),
            pltpu.VMEM((3, 4, 48, 128), BF16),
            pltpu.VMEM((2, 2304, 128), BF16),
            dma((2,)),
            dma((4, sends)),
            dma((4, sends)),
            dma((16,)),
            dma((16,)),
            dma((2, 8)),
            dma((2, 8)),
            dma((2,)),
            dma((2,)),
            dma((5, 3, 3)),
            dma((5, 3, 3)),
        ],
        compiler_params=pltpu.CompilerParams(
            collective_id=0, has_side_effects=True, vmem_limit_bytes=60 * 1024 * 1024
        ),
    )(
        box_class,
        box_offset.reshape(32),
        valid_count,
        feature_map,
        fpn_weight.reshape(2304, C),
        cot,
        head_weight.reshape(2304, C),
        deconv_weight.reshape(1024, C),
        mask_weight,
    )
    grad_weight = grad_weight.astype(F32).reshape(3, 3, C, C) / TOTAL
    return grad_input.reshape(32, 32, C), grad_weight


def solution(mesh):
    in_specs = (
        P("tile", "head", None),
        P(),
        P("head", None, None, None, None),
        P("head", None, None, None, None),
        P("head", None),
        P(("tile", "head")),
        P(("tile", "head"), None),
        P(("tile", "head")),
        P(("tile", "head"), None, None),
    )
    out_specs = (P("tile", "head", None), P())
    return jax.shard_map(local, mesh=mesh, in_specs=in_specs, out_specs=out_specs, check_vma=False)
```

```python
import functools

import jax
import jax.numpy as jnp
from jax import lax
from jax.experimental import pallas as pl
from jax.experimental.pallas import tpu as pltpu
from jax.sharding import PartitionSpec as P

MESH = pl.DeviceIdType.MESH
F32 = jnp.float32
BF16 = jnp.bfloat16

C = 256
HALF = 1680
ROWS = 2 * HALF
PIECES = ((0, 416), (416, 416), (832, 416), (1248, 432))
LAG = 2
PACE = 0.95
SLOTS = (
    (0, 0), (3, 0), (1, 0), (1, 3), (3, 1), (0, 1), (0, 3), (1, 1),
    (3, 3), (0, 2), (2, 0), (3, 2), (2, 3), (1, 2), (2, 1), (2, 2),
)
DIRS = ("x+", "x-", "z+", "z-")
TOTAL = 2048


def plan():
    def hop(d, plus):
        if d == 1:
            return 0, "+"
        if d == 3:
            return 0, "-"
        return (1, "+") if plus else (3, "-")

    left = {d: [] for d in DIRS}
    for q in range(4):
        plus = q % 2 == 0
        for slot in SLOTS[1:]:
            dz, dx = slot
            if (dz if q < 2 else not dx):
                before, sign = hop(dz, plus)
                left["z" + sign].append((q, (before, dx), slot))
            else:
                before, sign = hop(dx, plus)
                left["x" + sign].append((q, (dz, before), slot))
    rank = {s: i for i, s in enumerate(SLOTS)}
    ready = {(q, (0, 0)): 0 for q in range(4)}
    sends = []
    while any(left.values()):
        step = len(sends)
        now = []
        for d in DIRS:
            can = [e for e in left[d] if ready.get((e[0], e[1]), 99) <= step]
            if can:
                e = min(can, key=lambda e: rank[e[2]])
                left[d].remove(e)
                ready[(e[0], e[2])] = step + LAG
                now.append((DIRS.index(d), e[0], rank[e[1]], rank[e[2]]))
        sends.append(now)
    whole = [0] + [max(ready[(q, s)] for q in range(4)) for s in SLOTS[1:]]
    order = sorted(range(16), key=lambda i: whole[i])
    new = {old: i for i, old in enumerate(order)}
    sends = [[(d, q, new[a], new[b]) for d, q, a, b in now] for now in sends]
    return sends, [whole[i] for i in order], [SLOTS[i] for i in order]


SENDS, WHOLE, SLOTS = plan()
EARLY = 4
ENDS = [EARLY] + [max(WHOLE[p], int(6 + PACE * (p - 1))) for p in range(1, 16)]
ENDS = [min(e, len(SENDS) + LAG - 1) for e in ENDS]


def cdf_and_dens(v):
    e = jnp.exp2(v * v * (-0.5 * 1.4426950408889634))
    d = 1.0 + jnp.abs(v) * (0.3275911 * 0.7071067811865476)
    t = pl.reciprocal(d, approx=True)
    poly = t * (
        0.5 * 0.254829592
        + t
        * (
            0.5 * -0.284496736
            + t * (0.5 * 1.421413741 + t * (0.5 * -1.453152027 + t * (0.5 * 1.061405429)))
        )
    )
    tail = poly * e
    return jnp.where(v > 0, 1.0 - tail, tail), e


def dot(a, b):
    return lax.dot_general(a, b, (((1,), (0,)), ((), ())), preferred_element_type=F32)


def dot_t(a, b):
    return lax.dot_general(a, b, (((1,), (1,)), ((), ())), preferred_element_type=F32)


def fused_kernel(
    klass_ref, off_ref, count_ref, feat_ref, fpn_ref, cot_ref, head_ref, deconv_ref, mask_ref,
    gin_ref, gw_ref,
    wbuf, pyr, frame, fpx, fpt, xs, hidden, slope, total, dpre, grad, grad16,
    cols, rows_in, cols_in, corners_in,
    part, acc, core_in, send_a, in_a, acc_b, send_b, in_b, in_c, fin,
    own_sem, send_sem, recv_sem, sib_send, sib_recv, halo_send, halo_recv,
    core_send, core_recv, ring_send, ring_recv,
):
    t = lax.axis_index("tile")
    h = lax.axis_index("head")
    z, x = h // 4, h % 4
    y, core = t // 2, t % 2
    sibling = (t + 1 - 2 * core, h)
    there = (
        (t, z * 4 + (x + 1) % 4),
        (t, z * 4 + (x + 3) % 4),
        (t, (z + 1) % 4 * 4 + x),
        (t, (z + 3) % 4 * 4 + x),
    )
    up, down = (t + 7) % 8, (t + 1) % 8
    left, right = (h + 15) % 16, (h + 1) % 16
    coords = {"x": x, "y": y, "z": z}

    def peer(axis, c):
        if axis == "x":
            return (t, z * 4 + c)
        if axis == "z":
            return (t, c * 4 + x)
        return (c * 2 + core, h)

    base = pl.multiple_of(core * HALF, 16)
    other = pl.multiple_of((1 - core) * HALF, 16)

    own = (
        pltpu.make_async_copy(head_ref, wbuf.at[0, pl.ds(0, 2304)], own_sem.at[0]),
        pltpu.make_async_copy(deconv_ref, wbuf.at[0, pl.ds(2304, 1024)], own_sem.at[1]),
    )
    for c in own:
        c.start()
    barrier = pltpu.get_barrier_semaphore()
    greeted = [sibling, (up, h), (down, h), (t, left), (t, right)]
    greeted += [(a, b) for a in (up, down) for b in (left, right)]
    for axis in "xyz":
        greeted += [peer(axis, (coords[axis] + d) % 4) for d in (1, 2, 3)]
    for d in greeted:
        pl.semaphore_signal(barrier, inc=1, device_id=d, device_id_type=MESH)

    def piece(n, step):
        d, q, src, dst = SENDS[step][n]
        start, size = PIECES[q]
        rows = pl.ds(pl.multiple_of(base + start, 16), size)
        return pltpu.make_async_remote_copy(
            src_ref=wbuf.at[src, rows],
            dst_ref=wbuf.at[dst, rows],
            send_sem=send_sem.at[d, step],
            recv_sem=recv_sem.at[d, step],
            device_id=there[d],
            device_id_type=MESH,
        )

    def share(slot, mine):
        rows = pl.ds(base if mine else other, HALF)
        return pltpu.make_async_remote_copy(
            src_ref=wbuf.at[slot, rows],
            dst_ref=wbuf.at[slot, rows],
            send_sem=sib_send.at[slot],
            recv_sem=sib_recv.at[slot],
            device_id=sibling,
            device_id_type=MESH,
        )

    def traffic(step):
        if 0 <= step - LAG < len(SENDS):
            for n in range(len(SENDS[step - LAG])):
                piece(n, step - LAG).wait_recv()
        if step < len(SENDS):
            for n in range(len(SENDS[step])):
                piece(n, step).start()
        for slot in range(1, 16):
            if WHOLE[slot] == step:
                share(slot, True).start()

    def halo(k, src):
        sides = (
            (src.at[0], rows_in.at[k, 1], (up, h)),
            (src.at[31], rows_in.at[k, 0], (down, h)),
            (cols.at[k, 0], cols_in.at[k, 1], (t, left)),
            (cols.at[k, 1], cols_in.at[k, 0], (t, right)),
            (src.at[0, pl.ds(0, 16)], corners_in.at[k, 3], (up, left)),
            (src.at[0, pl.ds(16, 16)], corners_in.at[k, 2], (up, right)),
            (src.at[31, pl.ds(0, 16)], corners_in.at[k, 1], (down, left)),
            (src.at[31, pl.ds(16, 16)], corners_in.at[k, 0], (down, right)),
        )
        return [
            pltpu.make_async_remote_copy(
                src_ref=a,
                dst_ref=b,
                send_sem=halo_send.at[k, n],
                recv_sem=halo_recv.at[k, n],
                device_id=d,
                device_id_type=MESH,
            )
            for n, (a, b, d) in enumerate(sides)
        ]

    def place_tile(k, values):
        frame[1:33, 8:40, :] = values
        cols[k, 0] = values[:, 0, :].astype(BF16)
        cols[k, 1] = values[:, 31, :].astype(BF16)

    def place_halo(k):
        rows = [rows_in[k, n].astype(F32) for n in range(2)]
        sides = [cols_in[k, n].astype(F32) for n in range(2)]
        corners = [corners_in[k, n].astype(F32) for n in range(4)]
        frame[0, 8:40, :] = jnp.where(t > 0, rows[0], 0.0)
        frame[33, 8:40, :] = jnp.where(t < 7, rows[1], 0.0)
        frame[1:33, 7:8, :] = jnp.where(h > 0, sides[0], 0.0).reshape(32, 1, C)
        frame[1:33, 40:41, :] = jnp.where(h < 15, sides[1], 0.0).reshape(32, 1, C)
        frame[0, 7:8, :] = jnp.where((t > 0) & (h > 0), corners[0][15:16], 0.0)
        frame[0, 40:41, :] = jnp.where((t > 0) & (h < 15), corners[1][0:1], 0.0)
        frame[33, 7:8, :] = jnp.where((t < 7) & (h > 0), corners[2][15:16], 0.0)
        frame[33, 40:41, :] = jnp.where((t < 7) & (h < 15), corners[3][0:1], 0.0)
        for e in range(3):
            fpx[:, e * C : (e + 1) * C] = frame[:, 7 + e : 39 + e, :].reshape(1088, C).astype(BF16)

    place_tile(0, feat_ref[...].astype(F32))
    pl.semaphore_wait(barrier, len(greeted))
    halos = halo(0, feat_ref)
    for c in halos:
        c.start()
    wbuf[0, 3328:3360, :] = jnp.broadcast_to(mask_ref[...].astype(F32), (32, C)).astype(BF16)
    for c in own:
        c.wait()
    traffic(0)
    traffic(1)
    xs[...] = jnp.zeros_like(xs)
    grad[...] = jnp.zeros_like(grad)
    for c in halos:
        c.wait_recv()
    place_halo(0)
    traffic(2)
    for m in range(4):
        value = jnp.zeros((256, C), F32)
        for a in range(3):
            taps = fpx[a * 32 + m * 256 : a * 32 + (m + 1) * 256, :]
            value += dot(taps, fpn_ref[a * 3 * C : (a + 1) * 3 * C, :])
        pyr[m * 256 : (m + 1) * 256, :] = value.astype(BF16)
    traffic(3)
    for a in range(3):
        for e in range(3):
            fpt[(a * 3 + e) * C : (a * 3 + e + 1) * C, :] = jnp.transpose(
                fpx[a * 32 : a * 32 + 1024, e * C : (e + 1) * C]
            )

    def widen(b, value):
        xs[b, 16:240, C : 2 * C] = value.astype(BF16)
        xs[b, 16:240, 0:C] = pltpu.roll(value, 1, 0).astype(BF16)
        xs[b, 16:240, 2 * C :] = pltpu.roll(value, 223, 0).astype(BF16)

    def compute(p):
        dz = jnp.int32(0)
        dx = jnp.int32(0)
        for k in range(1, 16):
            dz = jnp.where(p == k, SLOTS[k][0], dz)
            dx = jnp.where(p == k, SLOTS[k][1], dx)
        klass = (z + 4 - dz) % 4 * 4 + (x + 4 - dx) % 4
        count = count_ref[0]
        slots = [jnp.int32(-1), jnp.int32(-1)]
        bases = [jnp.int32(-1), jnp.int32(-1)]
        for s in range(16):
            hit = (klass_ref[s] == klass) & (s < count)
            corner = off_ref[2 * s] * 32 + off_ref[2 * s + 1]
            again = hit & (slots[0] >= 0)
            only = hit & (slots[0] < 0)
            slots = [jnp.where(only, s, slots[0]), jnp.where(again, s, slots[1])]
            bases = [jnp.where(only, corner, bases[0]), jnp.where(again, corner, bases[1])]

        def places(axis):
            r = lax.broadcasted_iota(jnp.int32, (224, 1) if axis == 0 else (1, 224), axis)
            i, j = r // 16, r % 16
            spots = [jnp.where((j < 14) & (b >= 0), b + i * 32 + j, -1) for b in bases]
            return jnp.concatenate(spots, axis=axis)

        pixel = lax.broadcasted_iota(jnp.int32, (224, 1024), 1)
        spots = places(0)
        for b in range(2):
            pick = jnp.where(pixel == spots[b * 224 : (b + 1) * 224], 1.0, 0.0).astype(BF16)
            widen(b, dot(pick, pyr[...]))
        for b in range(2):
            rows = slice(b * 224, (b + 1) * 224)
            value = dot(xs[b, 0:224, :], wbuf[p, 0 : 3 * C, :])
            value += dot(xs[b, 16:240, :], wbuf[p, 3 * C : 6 * C, :])
            value += dot(xs[b, 32:256, :], wbuf[p, 6 * C : 9 * C, :])
            pre_one = value
            phi, e = cdf_and_dens(pre_one)
            hidden[rows, :] = (pre_one * phi).astype(BF16)
            slope[rows, :] = phi + pre_one * e * 0.3989422804014327
        gain = wbuf[p, 3328:3344, :][0:1].astype(F32)
        line = lax.broadcasted_iota(jnp.int32, (128, C), 0) % 64
        kernels = [wbuf[p, 2304 + q * C : 2304 + (q + 1) * C, :] for q in range(4)]
        for q in range(4):
            for b in range(2):
                rows = slice(b * 224, (b + 1) * 224)
                chosen = jnp.where((line == 4 * slots[b] + q) & (slots[b] >= 0), gain, 0.0)
                upper = dot(cot_ref[...], chosen.astype(BF16))
                pre_two = dot(hidden[rows, :], kernels[q])
                phi, e = cdf_and_dens(pre_two)
                value = upper * (phi + pre_two * e * 0.3989422804014327)
                dpre[rows, q * C : (q + 1) * C] = value.astype(BF16)
        for b in range(2):
            rows = slice(b * 224, (b + 1) * 224)
            value = dot_t(dpre[rows, 0:C], kernels[0])
            for q in range(1, 4):
                value += dot_t(dpre[rows, q * C : (q + 1) * C], kernels[q])
            widen(b, value * slope[rows, :])
        for b in range(2):
            value = jnp.zeros((224, C), F32)
            for a in range(3):
                for e in range(3):
                    tap = (2 - a) * 3 + 2 - e
                    value += dot_t(
                        xs[b, a * 16 : a * 16 + 224, e * C : (e + 1) * C],
                        wbuf[p, tap * C : (tap + 1) * C, :],
                    )
            total[b * 224 : (b + 1) * 224, :] = value.astype(BF16)
        pixel = lax.broadcasted_iota(jnp.int32, (1024, 448), 0)
        spread = jnp.where(pixel == places(1), 1.0, 0.0).astype(BF16)
        grad[...] += dot(spread, total[...])

    def advance(p):
        for step in range(EARLY if p == 0 else ENDS[p - 1] + 1, ENDS[p] + 1):
            traffic(step)
        if p > 0:
            share(p, False).wait_recv()

    def class_body(p, carry):
        for n in range(16):
            pl.when(p == n)(functools.partial(advance, n))
        compute(p)
        return carry

    lax.fori_loop(0, 16, class_body, 0)

    rounded = grad[...].astype(BF16)
    grad16[...] = rounded.reshape(32, 32, C)
    place_tile(1, grad16[...].astype(F32))
    halos_grad = halo(1, grad16)
    for c in halos_grad:
        c.start()
    for m in range(9):
        value = dot(fpt[m * C : (m + 1) * C, :], grad16[...].reshape(1024, C))
        rows = slice(m * C, (m + 1) * C)
        part[0, rows, :] = value[:, :128].astype(BF16)
        part[1, rows, :] = value[:, 128:].astype(BF16)
        acc[rows, :] = jnp.where(core == 0, value[:, :128], value[:, 128:])
    swap = pltpu.make_async_remote_copy(
        src_ref=part.at[1 - core],
        dst_ref=core_in,
        send_sem=core_send.at[0],
        recv_sem=core_recv.at[0],
        device_id=sibling,
        device_id_type=MESH,
    )
    swap.start()

    for c in halos_grad:
        c.wait_recv()
    place_halo(1)

    def back_conv(m):
        value = jnp.zeros((256, C), F32)
        for a in range(3):
            for e in range(3):
                taps = fpx[a * 32 + m * 256 : a * 32 + (m + 1) * 256, e * C : (e + 1) * C]
                tap = (2 - a) * 3 + 2 - e
                value += dot_t(taps, fpn_ref[tap * C : (tap + 1) * C, :])
        gin_ref[m * 256 : (m + 1) * 256, :] = value.astype(BF16)

    def ring(phase, g, d, axis, src, dst):
        return pltpu.make_async_remote_copy(
            src_ref=src,
            dst_ref=dst,
            send_sem=ring_send.at[phase, g, d - 1],
            recv_sem=ring_recv.at[phase, g, d - 1],
            device_id=peer(axis, (coords[axis] + d) % 4),
            device_id_type=MESH,
        )

    def span(start, size):
        return pl.ds(pl.multiple_of(start, 16), size)

    orders = ("yxz", "xzy", "zyx")
    groups = [(g, *[coords[a] for a in orders[g]]) for g in range(3)]

    swap.wait()
    for m in range(9):
        rows = slice(m * C, (m + 1) * C)
        value = acc[rows, :] + core_in[rows, :].astype(F32)
        acc[rows, :] = value
        send_a[rows, :] = value.astype(BF16)

    def out_a(g, ca, d):
        return ring(
            0, g, d, orders[g][0],
            send_a.at[span(768 * g + 192 * ((ca + d) % 4), 192)],
            in_a.at[g, ca],
        )

    def out_b(g, cb, d):
        return ring(1, g, d, orders[g][1], send_b.at[g, span(48 * ((cb + d) % 4), 48)], in_b.at[g, cb])

    def out_c(g, cc, d):
        return ring(2, g, d, orders[g][2], in_c.at[g, cc], in_c.at[g, cc])

    def back_b(g, ca, cb, d):
        rows = span(768 * g + 192 * ca + 48 * cb, 48)
        return ring(3, g, d, orders[g][1], fin.at[core, rows], fin.at[core, rows])

    def back_a(g, ca, d):
        rows = span(768 * g + 192 * ca, 192)
        return ring(4, g, d, orders[g][0], fin.at[core, rows], fin.at[core, rows])

    far = (1, 2, 3)
    for g, ca, cb, cc in groups:
        for d in far:
            out_a(g, ca, d).start()
    back_conv(0)
    for g, ca, cb, cc in groups:
        value = acc[span(768 * g + 192 * ca, 192), :]
        for d in far:
            out_a(g, (ca + 4 - d) % 4, d).wait_recv()
            value += in_a[g, (ca + 4 - d) % 4].astype(F32)
        acc_b[g] = value
        send_b[g] = value.astype(BF16)
        for d in far:
            out_b(g, cb, d).start()
    back_conv(1)
    for g, ca, cb, cc in groups:
        value = acc_b[g, span(48 * cb, 48), :]
        for d in far:
            out_b(g, (cb + 4 - d) % 4, d).wait_recv()
            value += in_b[g, (cb + 4 - d) % 4].astype(F32)
        in_c[g, cc] = value.astype(BF16)
        for d in far:
            out_c(g, cc, d).start()
    back_conv(2)
    for g, ca, cb, cc in groups:
        for d in far:
            out_c(g, (cc + 4 - d) % 4, d).wait_recv()
        value = in_c[g, 0].astype(F32)
        for n in far:
            value += in_c[g, n].astype(F32)
        fin[core, span(768 * g + 192 * ca + 48 * cb, 48), :] = value.astype(BF16)
        for d in far:
            back_b(g, ca, cb, d).start()
    back_conv(3)
    for g, ca, cb, cc in groups:
        for d in far:
            back_b(g, ca, (cb + 4 - d) % 4, d).wait_recv()
        for d in far:
            back_a(g, ca, d).start()
    for g, ca, cb, cc in groups:
        for d in far:
            back_a(g, (ca + 4 - d) % 4, d).wait_recv()

    def mirror(mine):
        half = fin.at[core if mine else 1 - core]
        return pltpu.make_async_remote_copy(
            src_ref=half,
            dst_ref=half,
            send_sem=core_send.at[1],
            recv_sem=core_recv.at[1],
            device_id=sibling,
            device_id_type=MESH,
        )

    mirror(True).start()
    for step in range(len(SENDS)):
        for n in range(len(SENDS[step])):
            piece(n, step).wait_send()
    for slot in range(1, 16):
        share(slot, True).wait_send()
    for c in (*halos, *halos_grad):
        c.wait_send()
    for g, ca, cb, cc in groups:
        for d in far:
            out_a(g, ca, d).wait_send()
            out_b(g, cb, d).wait_send()
            out_c(g, cc, d).wait_send()
            back_b(g, ca, cb, d).wait_send()
            back_a(g, ca, d).wait_send()
    mirror(True).wait_send()
    mirror(False).wait_recv()
    gw_ref[:, :128] = fin[0]
    gw_ref[:, 128:] = fin[1]


def local(
    feature_map,
    fpn_weight,
    head_weight,
    deconv_weight,
    mask_weight,
    box_class,
    box_offset,
    valid_count,
    mask_cotangent,
):
    cot = mask_cotangent.reshape(16, 14, 2, 14, 2).transpose(1, 3, 0, 2, 4).reshape(14, 14, 64)
    cot = jnp.pad(cot, ((0, 0), (0, 2), (0, 0))).reshape(224, 64)
    high = cot.astype(BF16)
    cot = jnp.concatenate([high, (cot - high.astype(F32)).astype(BF16)], axis=1)
    smem = pl.BlockSpec(memory_space=pltpu.SMEM)
    vmem = pl.BlockSpec(memory_space=pltpu.VMEM)
    hbm = pl.BlockSpec(memory_space=pl.ANY)
    sends = len(SENDS)
    dma = pltpu.SemaphoreType.DMA
    grad_input, grad_weight = pl.pallas_call(
        fused_kernel,
        out_shape=(
            jax.ShapeDtypeStruct((1024, C), BF16),
            jax.ShapeDtypeStruct((2304, C), BF16),
        ),
        in_specs=[smem, smem, smem, vmem, vmem, vmem, hbm, hbm, vmem],
        out_specs=(vmem, vmem),
        scratch_shapes=[
            pltpu.VMEM((16, ROWS, C), BF16),
            pltpu.VMEM((1024, C), BF16),
            pltpu.VMEM((34, 48, C), F32),
            pltpu.VMEM((1088, 3 * C), BF16),
            pltpu.VMEM((2304, 1024), BF16),
            pltpu.VMEM((2, 256, 3 * C), BF16),
            pltpu.VMEM((448, C), BF16),
            pltpu.VMEM((448, C), F32),
            pltpu.VMEM((448, C), BF16),
            pltpu.VMEM((448, 4 * C), BF16),
            pltpu.VMEM((1024, C), F32),
            pltpu.VMEM((32, 32, C), BF16),
            pltpu.VMEM((2, 2, 32, C), BF16),
            pltpu.VMEM((2, 2, 32, C), BF16),
            pltpu.VMEM((2, 2, 32, C), BF16),
            pltpu.VMEM((2, 4, 16, C), BF16),
            pltpu.VMEM((2, 2304, 128), BF16),
            pltpu.VMEM((2304, 128), F32),
            pltpu.VMEM((2304, 128), BF16),
            pltpu.VMEM((2304, 128), BF16),
            pltpu.VMEM((3, 4, 192, 128), BF16),
            pltpu.VMEM((3, 192, 128), F32),
            pltpu.VMEM((3, 192, 128), BF16),
            pltpu.VMEM((3, 4, 48, 128), BF16),
            pltpu.VMEM((3, 4, 48, 128), BF16),
            pltpu.VMEM((2, 2304, 128), BF16),
            dma((2,)),
            dma((4, sends)),
            dma((4, sends)),
            dma((16,)),
            dma((16,)),
            dma((2, 8)),
            dma((2, 8)),
            dma((2,)),
            dma((2,)),
            dma((5, 3, 3)),
            dma((5, 3, 3)),
        ],
        compiler_params=pltpu.CompilerParams(
            collective_id=0, has_side_effects=True, vmem_limit_bytes=60 * 1024 * 1024
        ),
    )(
        box_class,
        box_offset.reshape(32),
        valid_count,
        feature_map,
        fpn_weight.reshape(2304, C),
        cot,
        head_weight.reshape(2304, C),
        deconv_weight.reshape(1024, C),
        mask_weight,
    )
    grad_weight = grad_weight.astype(F32).reshape(3, 3, C, C) / TOTAL
    return grad_input.reshape(32, 32, C), grad_weight


def solution(mesh):
    in_specs = (
        P("tile", "head", None),
        P(),
        P("head", None, None, None, None),
        P("head", None, None, None, None),
        P("head", None),
        P(("tile", "head")),
        P(("tile", "head"), None),
        P(("tile", "head")),
        P(("tile", "head"), None, None),
    )
    out_specs = (P("tile", "head", None), P())
    return jax.shard_map(local, mesh=mesh, in_specs=in_specs, out_specs=out_specs, check_vma=False)
```

```python
import functools

import jax
import jax.numpy as jnp
from jax import lax
from jax.experimental import pallas as pl
from jax.experimental.pallas import tpu as pltpu
from jax.sharding import PartitionSpec as P

MESH = pl.DeviceIdType.MESH
F32 = jnp.float32
BF16 = jnp.bfloat16

C = 256
HALF = 1680
ROWS = 2 * HALF
PIECES = ((0, 416), (416, 416), (832, 416), (1248, 432))
LAG = 2
PACE = 0.95
SLOTS = (
    (0, 0), (3, 0), (1, 0), (1, 3), (3, 1), (0, 1), (0, 3), (1, 1),
    (3, 3), (0, 2), (2, 0), (3, 2), (2, 3), (1, 2), (2, 1), (2, 2),
)
DIRS = ("x+", "x-", "z+", "z-")
TOTAL = 2048


def plan():
    def hop(d, plus):
        if d == 1:
            return 0, "+"
        if d == 3:
            return 0, "-"
        return (1, "+") if plus else (3, "-")

    left = {d: [] for d in DIRS}
    for q in range(4):
        plus = q % 2 == 0
        for slot in SLOTS[1:]:
            dz, dx = slot
            if (dz if q < 2 else not dx):
                before, sign = hop(dz, plus)
                left["z" + sign].append((q, (before, dx), slot))
            else:
                before, sign = hop(dx, plus)
                left["x" + sign].append((q, (dz, before), slot))
    rank = {s: i for i, s in enumerate(SLOTS)}
    ready = {(q, (0, 0)): 0 for q in range(4)}
    sends = []
    while any(left.values()):
        step = len(sends)
        now = []
        for d in DIRS:
            can = [e for e in left[d] if ready.get((e[0], e[1]), 99) <= step]
            if can:
                e = min(can, key=lambda e: rank[e[2]])
                left[d].remove(e)
                ready[(e[0], e[2])] = step + LAG
                now.append((DIRS.index(d), e[0], rank[e[1]], rank[e[2]]))
        sends.append(now)
    whole = [0] + [max(ready[(q, s)] for q in range(4)) for s in SLOTS[1:]]
    order = sorted(range(16), key=lambda i: whole[i])
    new = {old: i for i, old in enumerate(order)}
    sends = [[(d, q, new[a], new[b]) for d, q, a, b in now] for now in sends]
    return sends, [whole[i] for i in order], [SLOTS[i] for i in order]


SENDS, WHOLE, SLOTS = plan()
EARLY = 4
ENDS = [EARLY] + [max(WHOLE[p], int(6 + PACE * (p - 1))) for p in range(1, 16)]
ENDS = [min(e, len(SENDS) + LAG - 1) for e in ENDS]


def cdf_and_dens(v):
    e = jnp.exp2(v * v * (-0.5 * 1.4426950408889634))
    d = 1.0 + jnp.abs(v) * (0.3275911 * 0.7071067811865476)
    t = pl.reciprocal(d, approx=True)
    poly = t * (
        0.5 * 0.254829592
        + t
        * (
            0.5 * -0.284496736
            + t * (0.5 * 1.421413741 + t * (0.5 * -1.453152027 + t * (0.5 * 1.061405429)))
        )
    )
    tail = poly * e
    return jnp.where(v > 0, 1.0 - tail, tail), e


def dot(a, b):
    return lax.dot_general(a, b, (((1,), (0,)), ((), ())), preferred_element_type=F32)


def dot_t(a, b):
    return lax.dot_general(a, b, (((1,), (1,)), ((), ())), preferred_element_type=F32)


def fused_kernel(
    klass_ref, off_ref, count_ref, feat_ref, fpn_ref, cot_ref, head_ref, deconv_ref, mask_ref,
    gin_ref, gw_ref,
    wbuf, pyr, frame, fpx, fpt, xs, ys, hidden, slope, total, dpre, grad, grad16,
    cols, rows_in, cols_in, corners_in,
    part, acc, core_in, send_a, in_a, acc_b, send_b, in_b, in_c, fin,
    own_sem, send_sem, recv_sem, sib_send, sib_recv, halo_send, halo_recv,
    core_send, core_recv, ring_send, ring_recv,
):
    t = lax.axis_index("tile")
    h = lax.axis_index("head")
    z, x = h // 4, h % 4
    y, core = t // 2, t % 2
    sibling = (t + 1 - 2 * core, h)
    there = (
        (t, z * 4 + (x + 1) % 4),
        (t, z * 4 + (x + 3) % 4),
        (t, (z + 1) % 4 * 4 + x),
        (t, (z + 3) % 4 * 4 + x),
    )
    up, down = (t + 7) % 8, (t + 1) % 8
    left, right = (h + 15) % 16, (h + 1) % 16
    coords = {"x": x, "y": y, "z": z}

    def peer(axis, c):
        if axis == "x":
            return (t, z * 4 + c)
        if axis == "z":
            return (t, c * 4 + x)
        return (c * 2 + core, h)

    base = pl.multiple_of(core * HALF, 16)
    other = pl.multiple_of((1 - core) * HALF, 16)

    own = (
        pltpu.make_async_copy(head_ref, wbuf.at[0, pl.ds(0, 2304)], own_sem.at[0]),
        pltpu.make_async_copy(deconv_ref, wbuf.at[0, pl.ds(2304, 1024)], own_sem.at[1]),
    )
    for c in own:
        c.start()
    barrier = pltpu.get_barrier_semaphore()
    greeted = [sibling, (up, h), (down, h), (t, left), (t, right)]
    greeted += [(a, b) for a in (up, down) for b in (left, right)]
    for axis in "xyz":
        greeted += [peer(axis, (coords[axis] + d) % 4) for d in (1, 2, 3)]
    for d in greeted:
        pl.semaphore_signal(barrier, inc=1, device_id=d, device_id_type=MESH)

    def piece(n, step):
        d, q, src, dst = SENDS[step][n]
        start, size = PIECES[q]
        rows = pl.ds(pl.multiple_of(base + start, 16), size)
        return pltpu.make_async_remote_copy(
            src_ref=wbuf.at[src, rows],
            dst_ref=wbuf.at[dst, rows],
            send_sem=send_sem.at[d, step],
            recv_sem=recv_sem.at[d, step],
            device_id=there[d],
            device_id_type=MESH,
        )

    def share(slot, mine):
        rows = pl.ds(base if mine else other, HALF)
        return pltpu.make_async_remote_copy(
            src_ref=wbuf.at[slot, rows],
            dst_ref=wbuf.at[slot, rows],
            send_sem=sib_send.at[slot],
            recv_sem=sib_recv.at[slot],
            device_id=sibling,
            device_id_type=MESH,
        )

    def traffic(step):
        if 0 <= step - LAG < len(SENDS):
            for n in range(len(SENDS[step - LAG])):
                piece(n, step - LAG).wait_recv()
        if step < len(SENDS):
            for n in range(len(SENDS[step])):
                piece(n, step).start()
        for slot in range(1, 16):
            if WHOLE[slot] == step:
                share(slot, True).start()

    def halo(k, src):
        sides = (
            (src.at[0], rows_in.at[k, 1], (up, h)),
            (src.at[31], rows_in.at[k, 0], (down, h)),
            (cols.at[k, 0], cols_in.at[k, 1], (t, left)),
            (cols.at[k, 1], cols_in.at[k, 0], (t, right)),
            (src.at[0, pl.ds(0, 16)], corners_in.at[k, 3], (up, left)),
            (src.at[0, pl.ds(16, 16)], corners_in.at[k, 2], (up, right)),
            (src.at[31, pl.ds(0, 16)], corners_in.at[k, 1], (down, left)),
            (src.at[31, pl.ds(16, 16)], corners_in.at[k, 0], (down, right)),
        )
        return [
            pltpu.make_async_remote_copy(
                src_ref=a,
                dst_ref=b,
                send_sem=halo_send.at[k, n],
                recv_sem=halo_recv.at[k, n],
                device_id=d,
                device_id_type=MESH,
            )
            for n, (a, b, d) in enumerate(sides)
        ]

    def place_tile(k, values):
        frame[1:33, 8:40, :] = values
        cols[k, 0] = values[:, 0, :].astype(BF16)
        cols[k, 1] = values[:, 31, :].astype(BF16)

    def place_halo(k):
        rows = [rows_in[k, n].astype(F32) for n in range(2)]
        sides = [cols_in[k, n].astype(F32) for n in range(2)]
        corners = [corners_in[k, n].astype(F32) for n in range(4)]
        frame[0, 8:40, :] = jnp.where(t > 0, rows[0], 0.0)
        frame[33, 8:40, :] = jnp.where(t < 7, rows[1], 0.0)
        frame[1:33, 7:8, :] = jnp.where(h > 0, sides[0], 0.0).reshape(32, 1, C)
        frame[1:33, 40:41, :] = jnp.where(h < 15, sides[1], 0.0).reshape(32, 1, C)
        frame[0, 7:8, :] = jnp.where((t > 0) & (h > 0), corners[0][15:16], 0.0)
        frame[0, 40:41, :] = jnp.where((t > 0) & (h < 15), corners[1][0:1], 0.0)
        frame[33, 7:8, :] = jnp.where((t < 7) & (h > 0), corners[2][15:16], 0.0)
        frame[33, 40:41, :] = jnp.where((t < 7) & (h < 15), corners[3][0:1], 0.0)
        for e in range(3):
            fpx[:, e * C : (e + 1) * C] = frame[:, 7 + e : 39 + e, :].reshape(1088, C).astype(BF16)

    place_tile(0, feat_ref[...].astype(F32))
    pl.semaphore_wait(barrier, len(greeted))
    halos = halo(0, feat_ref)
    for c in halos:
        c.start()
    wbuf[0, 3328:3360, :] = jnp.broadcast_to(mask_ref[...].astype(F32), (32, C)).astype(BF16)
    for c in own:
        c.wait()
    traffic(0)
    traffic(1)
    xs[...] = jnp.zeros_like(xs)
    ys[...] = jnp.zeros_like(ys)
    total[...] = jnp.zeros_like(total)
    grad[...] = jnp.zeros_like(grad)
    for c in halos:
        c.wait_recv()
    place_halo(0)
    traffic(2)
    for m in range(4):
        value = jnp.zeros((256, C), F32)
        for a in range(3):
            taps = fpx[a * 32 + m * 256 : a * 32 + (m + 1) * 256, :]
            value += dot(taps, fpn_ref[a * 3 * C : (a + 1) * 3 * C, :])
        pyr[m * 256 : (m + 1) * 256, :] = value.astype(BF16)
    traffic(3)
    for a in range(3):
        for e in range(3):
            fpt[(a * 3 + e) * C : (a * 3 + e + 1) * C, :] = jnp.transpose(
                fpx[a * 32 : a * 32 + 1024, e * C : (e + 1) * C]
            )

    def widen(ref, b, value):
        ref[b, 16:240, C : 2 * C] = value.astype(BF16)
        ref[b, 16:240, 0:C] = pltpu.roll(value, 1, 0).astype(BF16)
        ref[b, 16:240, 2 * C :] = pltpu.roll(value, 223, 0).astype(BF16)

    def find(p):
        dz = jnp.int32(0)
        dx = jnp.int32(0)
        for k in range(1, 16):
            dz = jnp.where(p == k, SLOTS[k][0], dz)
            dx = jnp.where(p == k, SLOTS[k][1], dx)
        klass = (z + 4 - dz) % 4 * 4 + (x + 4 - dx) % 4
        count = count_ref[0]
        slots = [jnp.int32(-1), jnp.int32(-1)]
        bases = [jnp.int32(-1), jnp.int32(-1)]
        for s in range(16):
            hit = (klass_ref[s] == klass) & (s < count)
            corner = off_ref[2 * s] * 32 + off_ref[2 * s + 1]
            again = hit & (slots[0] >= 0)
            only = hit & (slots[0] < 0)
            slots = [jnp.where(only, s, slots[0]), jnp.where(again, s, slots[1])]
            bases = [jnp.where(only, corner, bases[0]), jnp.where(again, corner, bases[1])]
        return (*slots, *bases)

    def places(base, axis):
        r = lax.broadcasted_iota(jnp.int32, (224, 1) if axis == 0 else (1, 224), axis)
        i, j = r // 16, r % 16
        return jnp.where((j < 14) & (base >= 0), base + i * 32 + j, -1)

    def crop(b, base):
        pixel = lax.broadcasted_iota(jnp.int32, (224, 1024), 1)
        pick = jnp.where(pixel == places(base, 0), 1.0, 0.0).astype(BF16)
        widen(xs, b, dot(pick, pyr[...]))

    def scatter(m, bases):
        pixel = lax.broadcasted_iota(jnp.int32, (256, 448), 0) + m * 256
        spots = jnp.concatenate([places(base, 1) for base in bases], axis=1)
        spread = jnp.where(pixel == spots, 1.0, 0.0).astype(BF16)
        grad[m * 256 : (m + 1) * 256, :] += dot(spread, total[...])

    def compute(p, carry):
        slots, bases, gone = carry[0:2], carry[2:4], carry[4:6]
        later = find(p + 1)
        for b in range(2):
            rows = slice(b * 224, (b + 1) * 224)
            value = dot(xs[b, 0:224, :], wbuf[p, 0 : 3 * C, :])
            value += dot(xs[b, 16:240, :], wbuf[p, 3 * C : 6 * C, :])
            value += dot(xs[b, 32:256, :], wbuf[p, 6 * C : 9 * C, :])
            pre_one = value
            phi, e = cdf_and_dens(pre_one)
            hidden[rows, :] = (pre_one * phi).astype(BF16)
            slope[rows, :] = phi + pre_one * e * 0.3989422804014327
        gain = wbuf[p, 3328:3344, :][0:1].astype(F32)
        line = lax.broadcasted_iota(jnp.int32, (128, C), 0) % 64
        kernels = [wbuf[p, 2304 + q * C : 2304 + (q + 1) * C, :] for q in range(4)]
        for q in range(4):
            for b in range(2):
                rows = slice(b * 224, (b + 1) * 224)
                chosen = jnp.where((line == 4 * slots[b] + q) & (slots[b] >= 0), gain, 0.0)
                upper = dot(cot_ref[...], chosen.astype(BF16))
                pre_two = dot(hidden[rows, :], kernels[q])
                phi, e = cdf_and_dens(pre_two)
                value = upper * (phi + pre_two * e * 0.3989422804014327)
                dpre[rows, q * C : (q + 1) * C] = value.astype(BF16)
                if b == 0:
                    scatter(q, gone)
                elif q % 2 == 1:
                    crop(q // 2, later[2 + q // 2])
        for b in range(2):
            rows = slice(b * 224, (b + 1) * 224)
            value = dot_t(dpre[rows, 0:C], kernels[0])
            for q in range(1, 4):
                value += dot_t(dpre[rows, q * C : (q + 1) * C], kernels[q])
            widen(ys, b, value * slope[rows, :])
        for b in range(2):
            value = jnp.zeros((224, C), F32)
            for a in range(3):
                for e in range(3):
                    tap = (2 - a) * 3 + 2 - e
                    value += dot_t(
                        ys[b, a * 16 : a * 16 + 224, e * C : (e + 1) * C],
                        wbuf[p, tap * C : (tap + 1) * C, :],
                    )
            total[b * 224 : (b + 1) * 224, :] = value.astype(BF16)
        return (*later, *bases)

    def advance(p):
        for step in range(EARLY if p == 0 else ENDS[p - 1] + 1, ENDS[p] + 1):
            traffic(step)
        if p > 0:
            share(p, False).wait_recv()

    def class_body(p, carry):
        for n in range(16):
            pl.when(p == n)(functools.partial(advance, n))
        return compute(p, carry)

    begin = find(0)
    for b in range(2):
        crop(b, begin[2 + b])
    none = jnp.int32(-1)
    ended = lax.fori_loop(0, 16, class_body, (*begin, none, none))
    for m in range(4):
        scatter(m, ended[4:6])

    rounded = grad[...].astype(BF16)
    grad16[...] = rounded.reshape(32, 32, C)
    place_tile(1, grad16[...].astype(F32))
    halos_grad = halo(1, grad16)
    for c in halos_grad:
        c.start()
    for m in range(9):
        value = dot(fpt[m * C : (m + 1) * C, :], grad16[...].reshape(1024, C))
        rows = slice(m * C, (m + 1) * C)
        part[0, rows, :] = value[:, :128].astype(BF16)
        part[1, rows, :] = value[:, 128:].astype(BF16)
        acc[rows, :] = jnp.where(core == 0, value[:, :128], value[:, 128:])
    swap = pltpu.make_async_remote_copy(
        src_ref=part.at[1 - core],
        dst_ref=core_in,
        send_sem=core_send.at[0],
        recv_sem=core_recv.at[0],
        device_id=sibling,
        device_id_type=MESH,
    )
    swap.start()

    for c in halos_grad:
        c.wait_recv()
    place_halo(1)

    def back_conv(m):
        value = jnp.zeros((256, C), F32)
        for a in range(3):
            for e in range(3):
                taps = fpx[a * 32 + m * 256 : a * 32 + (m + 1) * 256, e * C : (e + 1) * C]
                tap = (2 - a) * 3 + 2 - e
                value += dot_t(taps, fpn_ref[tap * C : (tap + 1) * C, :])
        gin_ref[m * 256 : (m + 1) * 256, :] = value.astype(BF16)

    def ring(phase, g, d, axis, src, dst):
        return pltpu.make_async_remote_copy(
            src_ref=src,
            dst_ref=dst,
            send_sem=ring_send.at[phase, g, d - 1],
            recv_sem=ring_recv.at[phase, g, d - 1],
            device_id=peer(axis, (coords[axis] + d) % 4),
            device_id_type=MESH,
        )

    def span(start, size):
        return pl.ds(pl.multiple_of(start, 16), size)

    orders = ("yxz", "xzy", "zyx")
    groups = [(g, *[coords[a] for a in orders[g]]) for g in range(3)]

    swap.wait()
    for m in range(9):
        rows = slice(m * C, (m + 1) * C)
        value = acc[rows, :] + core_in[rows, :].astype(F32)
        acc[rows, :] = value
        send_a[rows, :] = value.astype(BF16)

    def out_a(g, ca, d):
        return ring(
            0, g, d, orders[g][0],
            send_a.at[span(768 * g + 192 * ((ca + d) % 4), 192)],
            in_a.at[g, ca],
        )

    def out_b(g, cb, d):
        return ring(1, g, d, orders[g][1], send_b.at[g, span(48 * ((cb + d) % 4), 48)], in_b.at[g, cb])

    def out_c(g, cc, d):
        return ring(2, g, d, orders[g][2], in_c.at[g, cc], in_c.at[g, cc])

    def back_b(g, ca, cb, d):
        rows = span(768 * g + 192 * ca + 48 * cb, 48)
        return ring(3, g, d, orders[g][1], fin.at[core, rows], fin.at[core, rows])

    def back_a(g, ca, d):
        rows = span(768 * g + 192 * ca, 192)
        return ring(4, g, d, orders[g][0], fin.at[core, rows], fin.at[core, rows])

    far = (1, 2, 3)
    for g, ca, cb, cc in groups:
        for d in far:
            out_a(g, ca, d).start()
    back_conv(0)
    for g, ca, cb, cc in groups:
        value = acc[span(768 * g + 192 * ca, 192), :]
        for d in far:
            out_a(g, (ca + 4 - d) % 4, d).wait_recv()
            value += in_a[g, (ca + 4 - d) % 4].astype(F32)
        acc_b[g] = value
        send_b[g] = value.astype(BF16)
        for d in far:
            out_b(g, cb, d).start()
    back_conv(1)
    for g, ca, cb, cc in groups:
        value = acc_b[g, span(48 * cb, 48), :]
        for d in far:
            out_b(g, (cb + 4 - d) % 4, d).wait_recv()
            value += in_b[g, (cb + 4 - d) % 4].astype(F32)
        in_c[g, cc] = value.astype(BF16)
        for d in far:
            out_c(g, cc, d).start()
    back_conv(2)
    for g, ca, cb, cc in groups:
        for d in far:
            out_c(g, (cc + 4 - d) % 4, d).wait_recv()
        value = in_c[g, 0].astype(F32)
        for n in far:
            value += in_c[g, n].astype(F32)
        fin[core, span(768 * g + 192 * ca + 48 * cb, 48), :] = value.astype(BF16)
        for d in far:
            back_b(g, ca, cb, d).start()
    back_conv(3)
    for g, ca, cb, cc in groups:
        for d in far:
            back_b(g, ca, (cb + 4 - d) % 4, d).wait_recv()
        for d in far:
            back_a(g, ca, d).start()
    for g, ca, cb, cc in groups:
        for d in far:
            back_a(g, (ca + 4 - d) % 4, d).wait_recv()

    def mirror(mine):
        half = fin.at[core if mine else 1 - core]
        return pltpu.make_async_remote_copy(
            src_ref=half,
            dst_ref=half,
            send_sem=core_send.at[1],
            recv_sem=core_recv.at[1],
            device_id=sibling,
            device_id_type=MESH,
        )

    mirror(True).start()
    for step in range(len(SENDS)):
        for n in range(len(SENDS[step])):
            piece(n, step).wait_send()
    for slot in range(1, 16):
        share(slot, True).wait_send()
    for c in (*halos, *halos_grad):
        c.wait_send()
    for g, ca, cb, cc in groups:
        for d in far:
            out_a(g, ca, d).wait_send()
            out_b(g, cb, d).wait_send()
            out_c(g, cc, d).wait_send()
            back_b(g, ca, cb, d).wait_send()
            back_a(g, ca, d).wait_send()
    mirror(True).wait_send()
    mirror(False).wait_recv()
    gw_ref[:, :128] = fin[0]
    gw_ref[:, 128:] = fin[1]


def local(
    feature_map,
    fpn_weight,
    head_weight,
    deconv_weight,
    mask_weight,
    box_class,
    box_offset,
    valid_count,
    mask_cotangent,
):
    cot = mask_cotangent.reshape(16, 14, 2, 14, 2).transpose(1, 3, 0, 2, 4).reshape(14, 14, 64)
    cot = jnp.pad(cot, ((0, 0), (0, 2), (0, 0))).reshape(224, 64)
    high = cot.astype(BF16)
    cot = jnp.concatenate([high, (cot - high.astype(F32)).astype(BF16)], axis=1)
    smem = pl.BlockSpec(memory_space=pltpu.SMEM)
    vmem = pl.BlockSpec(memory_space=pltpu.VMEM)
    hbm = pl.BlockSpec(memory_space=pl.ANY)
    sends = len(SENDS)
    dma = pltpu.SemaphoreType.DMA
    grad_input, grad_weight = pl.pallas_call(
        fused_kernel,
        out_shape=(
            jax.ShapeDtypeStruct((1024, C), BF16),
            jax.ShapeDtypeStruct((2304, C), BF16),
        ),
        in_specs=[smem, smem, smem, vmem, vmem, vmem, hbm, hbm, vmem],
        out_specs=(vmem, vmem),
        scratch_shapes=[
            pltpu.VMEM((16, ROWS, C), BF16),
            pltpu.VMEM((1024, C), BF16),
            pltpu.VMEM((34, 48, C), F32),
            pltpu.VMEM((1088, 3 * C), BF16),
            pltpu.VMEM((2304, 1024), BF16),
            pltpu.VMEM((2, 256, 3 * C), BF16),
            pltpu.VMEM((2, 256, 3 * C), BF16),
            pltpu.VMEM((448, C), BF16),
            pltpu.VMEM((448, C), F32),
            pltpu.VMEM((448, C), BF16),
            pltpu.VMEM((448, 4 * C), BF16),
            pltpu.VMEM((1024, C), F32),
            pltpu.VMEM((32, 32, C), BF16),
            pltpu.VMEM((2, 2, 32, C), BF16),
            pltpu.VMEM((2, 2, 32, C), BF16),
            pltpu.VMEM((2, 2, 32, C), BF16),
            pltpu.VMEM((2, 4, 16, C), BF16),
            pltpu.VMEM((2, 2304, 128), BF16),
            pltpu.VMEM((2304, 128), F32),
            pltpu.VMEM((2304, 128), BF16),
            pltpu.VMEM((2304, 128), BF16),
            pltpu.VMEM((3, 4, 192, 128), BF16),
            pltpu.VMEM((3, 192, 128), F32),
            pltpu.VMEM((3, 192, 128), BF16),
            pltpu.VMEM((3, 4, 48, 128), BF16),
            pltpu.VMEM((3, 4, 48, 128), BF16),
            pltpu.VMEM((2, 2304, 128), BF16),
            dma((2,)),
            dma((4, sends)),
            dma((4, sends)),
            dma((16,)),
            dma((16,)),
            dma((2, 8)),
            dma((2, 8)),
            dma((2,)),
            dma((2,)),
            dma((5, 3, 3)),
            dma((5, 3, 3)),
        ],
        compiler_params=pltpu.CompilerParams(
            collective_id=0, has_side_effects=True, vmem_limit_bytes=60 * 1024 * 1024
        ),
    )(
        box_class,
        box_offset.reshape(32),
        valid_count,
        feature_map,
        fpn_weight.reshape(2304, C),
        cot,
        head_weight.reshape(2304, C),
        deconv_weight.reshape(1024, C),
        mask_weight,
    )
    grad_weight = grad_weight.astype(F32).reshape(3, 3, C, C) / TOTAL
    return grad_input.reshape(32, 32, C), grad_weight


def solution(mesh):
    in_specs = (
        P("tile", "head", None),
        P(),
        P("head", None, None, None, None),
        P("head", None, None, None, None),
        P("head", None),
        P(("tile", "head")),
        P(("tile", "head"), None),
        P(("tile", "head")),
        P(("tile", "head"), None, None),
    )
    out_specs = (P("tile", "head", None), P())
    return jax.shard_map(local, mesh=mesh, in_specs=in_specs, out_specs=out_specs, check_vma=False)
```

```python
import functools

import jax
import jax.numpy as jnp
from jax import lax
from jax.experimental import pallas as pl
from jax.experimental.pallas import tpu as pltpu
from jax.sharding import PartitionSpec as P

MESH = pl.DeviceIdType.MESH
F32 = jnp.float32
BF16 = jnp.bfloat16

C = 256
HALF = 1680
ROWS = 2 * HALF
PIECES = ((0, 416), (416, 416), (832, 416), (1248, 432))
LAG = 2
PACE = 0.95
SLOTS = (
    (0, 0), (3, 0), (1, 0), (1, 3), (3, 1), (0, 1), (0, 3), (1, 1),
    (3, 3), (0, 2), (2, 0), (3, 2), (2, 3), (1, 2), (2, 1), (2, 2),
)
DIRS = ("x+", "x-", "z+", "z-")
TOTAL = 2048


def plan():
    def hop(d, plus):
        if d == 1:
            return 0, "+"
        if d == 3:
            return 0, "-"
        return (1, "+") if plus else (3, "-")

    left = {d: [] for d in DIRS}
    for q in range(4):
        plus = q % 2 == 0
        for slot in SLOTS[1:]:
            dz, dx = slot
            if (dz if q < 2 else not dx):
                before, sign = hop(dz, plus)
                left["z" + sign].append((q, (before, dx), slot))
            else:
                before, sign = hop(dx, plus)
                left["x" + sign].append((q, (dz, before), slot))
    rank = {s: i for i, s in enumerate(SLOTS)}
    ready = {(q, (0, 0)): 0 for q in range(4)}
    sends = []
    while any(left.values()):
        step = len(sends)
        now = []
        for d in DIRS:
            can = [e for e in left[d] if ready.get((e[0], e[1]), 99) <= step]
            if can:
                e = min(can, key=lambda e: rank[e[2]])
                left[d].remove(e)
                ready[(e[0], e[2])] = step + LAG
                now.append((DIRS.index(d), e[0], rank[e[1]], rank[e[2]]))
        sends.append(now)
    whole = [0] + [max(ready[(q, s)] for q in range(4)) for s in SLOTS[1:]]
    order = sorted(range(16), key=lambda i: whole[i])
    new = {old: i for i, old in enumerate(order)}
    sends = [[(d, q, new[a], new[b]) for d, q, a, b in now] for now in sends]
    return sends, [whole[i] for i in order], [SLOTS[i] for i in order]


SENDS, WHOLE, SLOTS = plan()
EARLY = 4
ENDS = [EARLY] + [max(WHOLE[p], int(6 + PACE * (p - 1))) for p in range(1, 16)]
ENDS = [min(e, len(SENDS) + LAG - 1) for e in ENDS]


def cdf_and_dens(v):
    e = jnp.exp2(v * v * (-0.5 * 1.4426950408889634))
    d = 1.0 + jnp.abs(v) * (0.3275911 * 0.7071067811865476)
    t = pl.reciprocal(d, approx=True)
    poly = t * (
        0.5 * 0.254829592
        + t
        * (
            0.5 * -0.284496736
            + t * (0.5 * 1.421413741 + t * (0.5 * -1.453152027 + t * (0.5 * 1.061405429)))
        )
    )
    tail = poly * e
    return jnp.where(v > 0, 1.0 - tail, tail), e


def dot(a, b):
    return lax.dot_general(a, b, (((1,), (0,)), ((), ())), preferred_element_type=F32)


def dot_t(a, b):
    return lax.dot_general(a, b, (((1,), (1,)), ((), ())), preferred_element_type=F32)


def fused_kernel(
    klass_ref, off_ref, count_ref, feat_ref, fpn_ref, cot_ref, head_ref, deconv_ref, mask_ref,
    gin_ref, gw_ref,
    wbuf, pyr, frame, fpx, fpt, xs, ys, hidden, slope, total, dpre, grad, grad16,
    cols, rows_in, cols_in, corners_in,
    part, acc, core_in, send_a, in_a, acc_b, send_b, in_b, in_c, fin,
    own_sem, send_sem, recv_sem, sib_send, sib_recv, halo_send, halo_recv,
    core_send, core_recv, ring_send, ring_recv,
):
    t = lax.axis_index("tile")
    h = lax.axis_index("head")
    z, x = h // 4, h % 4
    y, core = t // 2, t % 2
    sibling = (t + 1 - 2 * core, h)
    there = (
        (t, z * 4 + (x + 1) % 4),
        (t, z * 4 + (x + 3) % 4),
        (t, (z + 1) % 4 * 4 + x),
        (t, (z + 3) % 4 * 4 + x),
    )
    up, down = (t + 7) % 8, (t + 1) % 8
    left, right = (h + 15) % 16, (h + 1) % 16
    coords = {"x": x, "y": y, "z": z}

    def peer(axis, c):
        if axis == "x":
            return (t, z * 4 + c)
        if axis == "z":
            return (t, c * 4 + x)
        return (c * 2 + core, h)

    base = pl.multiple_of(core * HALF, 16)
    other = pl.multiple_of((1 - core) * HALF, 16)

    own = (
        pltpu.make_async_copy(head_ref, wbuf.at[0, pl.ds(0, 2304)], own_sem.at[0]),
        pltpu.make_async_copy(deconv_ref, wbuf.at[0, pl.ds(2304, 1024)], own_sem.at[1]),
    )
    for c in own:
        c.start()
    barrier = pltpu.get_barrier_semaphore()
    greeted = [sibling, (up, h), (down, h), (t, left), (t, right)]
    greeted += [(a, b) for a in (up, down) for b in (left, right)]
    for axis in "xyz":
        greeted += [peer(axis, (coords[axis] + d) % 4) for d in (1, 2, 3)]
    for d in greeted:
        pl.semaphore_signal(barrier, inc=1, device_id=d, device_id_type=MESH)

    def piece(n, step):
        d, q, src, dst = SENDS[step][n]
        start, size = PIECES[q]
        rows = pl.ds(pl.multiple_of(base + start, 16), size)
        return pltpu.make_async_remote_copy(
            src_ref=wbuf.at[src, rows],
            dst_ref=wbuf.at[dst, rows],
            send_sem=send_sem.at[d, step],
            recv_sem=recv_sem.at[d, step],
            device_id=there[d],
            device_id_type=MESH,
        )

    def share(slot, mine):
        rows = pl.ds(base if mine else other, HALF)
        return pltpu.make_async_remote_copy(
            src_ref=wbuf.at[slot, rows],
            dst_ref=wbuf.at[slot, rows],
            send_sem=sib_send.at[slot],
            recv_sem=sib_recv.at[slot],
            device_id=sibling,
            device_id_type=MESH,
        )

    def traffic(step):
        if 0 <= step - LAG < len(SENDS):
            for n in range(len(SENDS[step - LAG])):
                piece(n, step - LAG).wait_recv()
        if step < len(SENDS):
            for n in range(len(SENDS[step])):
                piece(n, step).start()
        for slot in range(1, 16):
            if WHOLE[slot] == step:
                share(slot, True).start()

    def halo(k, src):
        sides = (
            (src.at[0], rows_in.at[k, 1], (up, h)),
            (src.at[31], rows_in.at[k, 0], (down, h)),
            (cols.at[k, 0], cols_in.at[k, 1], (t, left)),
            (cols.at[k, 1], cols_in.at[k, 0], (t, right)),
            (src.at[0, pl.ds(0, 16)], corners_in.at[k, 3], (up, left)),
            (src.at[0, pl.ds(16, 16)], corners_in.at[k, 2], (up, right)),
            (src.at[31, pl.ds(0, 16)], corners_in.at[k, 1], (down, left)),
            (src.at[31, pl.ds(16, 16)], corners_in.at[k, 0], (down, right)),
        )
        return [
            pltpu.make_async_remote_copy(
                src_ref=a,
                dst_ref=b,
                send_sem=halo_send.at[k, n],
                recv_sem=halo_recv.at[k, n],
                device_id=d,
                device_id_type=MESH,
            )
            for n, (a, b, d) in enumerate(sides)
        ]

    def place_tile(k, values):
        frame[1:33, 8:40, :] = values
        cols[k, 0] = values[:, 0, :].astype(BF16)
        cols[k, 1] = values[:, 31, :].astype(BF16)

    def place_halo(k):
        rows = [rows_in[k, n].astype(F32) for n in range(2)]
        sides = [cols_in[k, n].astype(F32) for n in range(2)]
        corners = [corners_in[k, n].astype(F32) for n in range(4)]
        frame[0, 8:40, :] = jnp.where(t > 0, rows[0], 0.0)
        frame[33, 8:40, :] = jnp.where(t < 7, rows[1], 0.0)
        frame[1:33, 7:8, :] = jnp.where(h > 0, sides[0], 0.0).reshape(32, 1, C)
        frame[1:33, 40:41, :] = jnp.where(h < 15, sides[1], 0.0).reshape(32, 1, C)
        frame[0, 7:8, :] = jnp.where((t > 0) & (h > 0), corners[0][15:16], 0.0)
        frame[0, 40:41, :] = jnp.where((t > 0) & (h < 15), corners[1][0:1], 0.0)
        frame[33, 7:8, :] = jnp.where((t < 7) & (h > 0), corners[2][15:16], 0.0)
        frame[33, 40:41, :] = jnp.where((t < 7) & (h < 15), corners[3][0:1], 0.0)
        for e in range(3):
            fpx[:, e * C : (e + 1) * C] = frame[:, 7 + e : 39 + e, :].reshape(1088, C).astype(BF16)

    place_tile(0, feat_ref[...].astype(F32))
    pl.semaphore_wait(barrier, len(greeted))
    halos = halo(0, feat_ref)
    for c in halos:
        c.start()
    wbuf[0, 3328:3360, :] = jnp.broadcast_to(mask_ref[...].astype(F32), (32, C)).astype(BF16)
    for c in own:
        c.wait()
    traffic(0)
    traffic(1)
    xs[...] = jnp.zeros_like(xs)
    ys[...] = jnp.zeros_like(ys)
    total[...] = jnp.zeros_like(total)
    grad[...] = jnp.zeros_like(grad)
    for c in halos:
        c.wait_recv()
    place_halo(0)
    traffic(2)
    for m in range(4):
        value = jnp.zeros((256, C), F32)
        for a in range(3):
            taps = fpx[a * 32 + m * 256 : a * 32 + (m + 1) * 256, :]
            value += dot(taps, fpn_ref[a * 3 * C : (a + 1) * 3 * C, :])
        pyr[m * 256 : (m + 1) * 256, :] = value.astype(BF16)
    traffic(3)
    for a in range(3):
        for e in range(3):
            fpt[(a * 3 + e) * C : (a * 3 + e + 1) * C, :] = jnp.transpose(
                fpx[a * 32 : a * 32 + 1024, e * C : (e + 1) * C]
            )

    def widen(ref, b, value):
        ref[b, 16:240, C : 2 * C] = value.astype(BF16)
        ref[b, 16:240, 0:C] = pltpu.roll(value, 1, 0).astype(BF16)
        ref[b, 16:240, 2 * C :] = pltpu.roll(value, 223, 0).astype(BF16)

    def find(p):
        dz = jnp.int32(0)
        dx = jnp.int32(0)
        for k in range(1, 16):
            dz = jnp.where(p == k, SLOTS[k][0], dz)
            dx = jnp.where(p == k, SLOTS[k][1], dx)
        klass = (z + 4 - dz) % 4 * 4 + (x + 4 - dx) % 4
        count = count_ref[0]
        slots = [jnp.int32(-1), jnp.int32(-1)]
        bases = [jnp.int32(-1), jnp.int32(-1)]
        for s in range(16):
            hit = (klass_ref[s] == klass) & (s < count)
            corner = off_ref[s, 0] * 32 + off_ref[s, 1]
            again = hit & (slots[0] >= 0)
            only = hit & (slots[0] < 0)
            slots = [jnp.where(only, s, slots[0]), jnp.where(again, s, slots[1])]
            bases = [jnp.where(only, corner, bases[0]), jnp.where(again, corner, bases[1])]
        return (*slots, *bases)

    def places(base, axis):
        r = lax.broadcasted_iota(jnp.int32, (224, 1) if axis == 0 else (1, 224), axis)
        i, j = r // 16, r % 16
        return jnp.where((j < 14) & (base >= 0), base + i * 32 + j, -1)

    def crop(b, base):
        pixel = lax.broadcasted_iota(jnp.int32, (224, 1024), 1)
        pick = jnp.where(pixel == places(base, 0), 1.0, 0.0).astype(BF16)
        widen(xs, b, dot(pick, pyr[...]))

    def scatter(m, bases):
        pixel = lax.broadcasted_iota(jnp.int32, (256, 448), 0) + m * 256
        spots = jnp.concatenate([places(base, 1) for base in bases], axis=1)
        spread = jnp.where(pixel == spots, 1.0, 0.0).astype(BF16)
        grad[m * 256 : (m + 1) * 256, :] += dot(spread, total[...])

    def compute(p, carry):
        slots, bases, gone = carry[0:2], carry[2:4], carry[4:6]
        later = find(p + 1)
        for b in range(2):
            rows = slice(b * 224, (b + 1) * 224)
            value = dot(xs[b, 0:224, :], wbuf[p, 0 : 3 * C, :])
            value += dot(xs[b, 16:240, :], wbuf[p, 3 * C : 6 * C, :])
            value += dot(xs[b, 32:256, :], wbuf[p, 6 * C : 9 * C, :])
            pre_one = value
            phi, e = cdf_and_dens(pre_one)
            hidden[rows, :] = (pre_one * phi).astype(BF16)
            slope[rows, :] = phi + pre_one * e * 0.3989422804014327
        gain = wbuf[p, 3328:3344, :][0:1].astype(F32)
        line = lax.broadcasted_iota(jnp.int32, (128, C), 0) % 64
        kernels = [wbuf[p, 2304 + q * C : 2304 + (q + 1) * C, :] for q in range(4)]
        for q in range(4):
            for b in range(2):
                rows = slice(b * 224, (b + 1) * 224)
                chosen = jnp.where((line == 16 * q + slots[b]) & (slots[b] >= 0), gain, 0.0)
                upper = dot(cot_ref[...], chosen.astype(BF16))
                pre_two = dot(hidden[rows, :], kernels[q])
                phi, e = cdf_and_dens(pre_two)
                value = upper * (phi + pre_two * e * 0.3989422804014327)
                dpre[rows, q * C : (q + 1) * C] = value.astype(BF16)
                if b == 0:
                    scatter(q, gone)
                elif q % 2 == 1:
                    crop(q // 2, later[2 + q // 2])
        for b in range(2):
            rows = slice(b * 224, (b + 1) * 224)
            value = dot_t(dpre[rows, 0:C], kernels[0])
            for q in range(1, 4):
                value += dot_t(dpre[rows, q * C : (q + 1) * C], kernels[q])
            widen(ys, b, value * slope[rows, :])
        for b in range(2):
            value = jnp.zeros((224, C), F32)
            for a in range(3):
                for e in range(3):
                    tap = (2 - a) * 3 + 2 - e
                    value += dot_t(
                        ys[b, a * 16 : a * 16 + 224, e * C : (e + 1) * C],
                        wbuf[p, tap * C : (tap + 1) * C, :],
                    )
            total[b * 224 : (b + 1) * 224, :] = value.astype(BF16)
        return (*later, *bases)

    def advance(p):
        for step in range(EARLY if p == 0 else ENDS[p - 1] + 1, ENDS[p] + 1):
            traffic(step)
        if p > 0:
            share(p, False).wait_recv()

    def class_body(p, carry):
        for n in range(16):
            pl.when(p == n)(functools.partial(advance, n))
        return compute(p, carry)

    begin = find(0)
    for b in range(2):
        crop(b, begin[2 + b])
    none = jnp.int32(-1)
    ended = lax.fori_loop(0, 16, class_body, (*begin, none, none))
    for m in range(4):
        scatter(m, ended[4:6])

    rounded = grad[...].astype(BF16)
    grad16[...] = rounded.reshape(32, 32, C)
    place_tile(1, grad16[...].astype(F32))
    halos_grad = halo(1, grad16)
    for c in halos_grad:
        c.start()
    for m in range(9):
        value = dot(fpt[m * C : (m + 1) * C, :], grad16[...].reshape(1024, C))
        rows = slice(m * C, (m + 1) * C)
        part[0, rows, :] = value[:, :128].astype(BF16)
        part[1, rows, :] = value[:, 128:].astype(BF16)
        acc[rows, :] = jnp.where(core == 0, value[:, :128], value[:, 128:])
    swap = pltpu.make_async_remote_copy(
        src_ref=part.at[1 - core],
        dst_ref=core_in,
        send_sem=core_send.at[0],
        recv_sem=core_recv.at[0],
        device_id=sibling,
        device_id_type=MESH,
    )
    swap.start()

    for c in halos_grad:
        c.wait_recv()
    place_halo(1)

    def back_conv(m):
        value = jnp.zeros((256, C), F32)
        for a in range(3):
            for e in range(3):
                taps = fpx[a * 32 + m * 256 : a * 32 + (m + 1) * 256, e * C : (e + 1) * C]
                tap = (2 - a) * 3 + 2 - e
                value += dot_t(taps, fpn_ref[tap * C : (tap + 1) * C, :])
        gin_ref[m * 256 : (m + 1) * 256, :] = value.astype(BF16)

    def ring(phase, g, d, axis, src, dst):
        return pltpu.make_async_remote_copy(
            src_ref=src,
            dst_ref=dst,
            send_sem=ring_send.at[phase, g, d - 1],
            recv_sem=ring_recv.at[phase, g, d - 1],
            device_id=peer(axis, (coords[axis] + d) % 4),
            device_id_type=MESH,
        )

    def span(start, size):
        return pl.ds(pl.multiple_of(start, 16), size)

    orders = ("yxz", "xzy", "zyx")
    groups = [(g, *[coords[a] for a in orders[g]]) for g in range(3)]

    swap.wait()
    for m in range(9):
        rows = slice(m * C, (m + 1) * C)
        value = acc[rows, :] + core_in[rows, :].astype(F32)
        acc[rows, :] = value
        send_a[rows, :] = value.astype(BF16)

    def out_a(g, ca, d):
        return ring(
            0, g, d, orders[g][0],
            send_a.at[span(768 * g + 192 * ((ca + d) % 4), 192)],
            in_a.at[g, ca],
        )

    def out_b(g, cb, d):
        return ring(1, g, d, orders[g][1], send_b.at[g, span(48 * ((cb + d) % 4), 48)], in_b.at[g, cb])

    def out_c(g, cc, d):
        return ring(2, g, d, orders[g][2], in_c.at[g, cc], in_c.at[g, cc])

    def back_b(g, ca, cb, d):
        rows = span(768 * g + 192 * ca + 48 * cb, 48)
        return ring(3, g, d, orders[g][1], fin.at[core, rows], fin.at[core, rows])

    def back_a(g, ca, d):
        rows = span(768 * g + 192 * ca, 192)
        return ring(4, g, d, orders[g][0], fin.at[core, rows], fin.at[core, rows])

    far = (1, 2, 3)
    for g, ca, cb, cc in groups:
        for d in far:
            out_a(g, ca, d).start()
    back_conv(0)
    for g, ca, cb, cc in groups:
        value = acc[span(768 * g + 192 * ca, 192), :]
        for d in far:
            out_a(g, (ca + 4 - d) % 4, d).wait_recv()
            value += in_a[g, (ca + 4 - d) % 4].astype(F32)
        acc_b[g] = value
        send_b[g] = value.astype(BF16)
        for d in far:
            out_b(g, cb, d).start()
    back_conv(1)
    for g, ca, cb, cc in groups:
        value = acc_b[g, span(48 * cb, 48), :]
        for d in far:
            out_b(g, (cb + 4 - d) % 4, d).wait_recv()
            value += in_b[g, (cb + 4 - d) % 4].astype(F32)
        in_c[g, cc] = value.astype(BF16)
        for d in far:
            out_c(g, cc, d).start()
    back_conv(2)
    for g, ca, cb, cc in groups:
        for d in far:
            out_c(g, (cc + 4 - d) % 4, d).wait_recv()
        value = in_c[g, 0].astype(F32)
        for n in far:
            value += in_c[g, n].astype(F32)
        fin[core, span(768 * g + 192 * ca + 48 * cb, 48), :] = value.astype(BF16)
        for d in far:
            back_b(g, ca, cb, d).start()
    back_conv(3)
    for g, ca, cb, cc in groups:
        for d in far:
            back_b(g, ca, (cb + 4 - d) % 4, d).wait_recv()
        for d in far:
            back_a(g, ca, d).start()
    for g, ca, cb, cc in groups:
        for d in far:
            back_a(g, (ca + 4 - d) % 4, d).wait_recv()

    def mirror(mine):
        half = fin.at[core if mine else 1 - core]
        return pltpu.make_async_remote_copy(
            src_ref=half,
            dst_ref=half,
            send_sem=core_send.at[1],
            recv_sem=core_recv.at[1],
            device_id=sibling,
            device_id_type=MESH,
        )

    mirror(True).start()
    for step in range(len(SENDS)):
        for n in range(len(SENDS[step])):
            piece(n, step).wait_send()
    for slot in range(1, 16):
        share(slot, True).wait_send()
    for c in (*halos, *halos_grad):
        c.wait_send()
    for g, ca, cb, cc in groups:
        for d in far:
            out_a(g, ca, d).wait_send()
            out_b(g, cb, d).wait_send()
            out_c(g, cc, d).wait_send()
            back_b(g, ca, cb, d).wait_send()
            back_a(g, ca, d).wait_send()
    mirror(True).wait_send()
    mirror(False).wait_recv()
    gw_ref[:, :128] = fin[0]
    gw_ref[:, 128:] = fin[1]


def local(
    feature_map,
    fpn_weight,
    head_weight,
    deconv_weight,
    mask_weight,
    box_class,
    box_offset,
    valid_count,
    mask_cotangent,
):
    cot = mask_cotangent.reshape(16, 14, 2, 14, 2).transpose(1, 3, 2, 4, 0).reshape(14, 14, 64)
    cot = jnp.pad(cot, ((0, 0), (0, 2), (0, 0))).reshape(224, 64)
    high = cot.astype(BF16)
    cot = jnp.concatenate([high, (cot - high.astype(F32)).astype(BF16)], axis=1)
    smem = pl.BlockSpec(memory_space=pltpu.SMEM)
    vmem = pl.BlockSpec(memory_space=pltpu.VMEM)
    hbm = pl.BlockSpec(memory_space=pl.ANY)
    sends = len(SENDS)
    dma = pltpu.SemaphoreType.DMA
    grad_input, grad_weight = pl.pallas_call(
        fused_kernel,
        out_shape=(
            jax.ShapeDtypeStruct((1024, C), BF16),
            jax.ShapeDtypeStruct((2304, C), BF16),
        ),
        in_specs=[smem, smem, smem, vmem, vmem, vmem, hbm, hbm, vmem],
        out_specs=(vmem, vmem),
        scratch_shapes=[
            pltpu.VMEM((16, ROWS, C), BF16),
            pltpu.VMEM((1024, C), BF16),
            pltpu.VMEM((34, 48, C), F32),
            pltpu.VMEM((1088, 3 * C), BF16),
            pltpu.VMEM((2304, 1024), BF16),
            pltpu.VMEM((2, 256, 3 * C), BF16),
            pltpu.VMEM((2, 256, 3 * C), BF16),
            pltpu.VMEM((448, C), BF16),
            pltpu.VMEM((448, C), F32),
            pltpu.VMEM((448, C), BF16),
            pltpu.VMEM((448, 4 * C), BF16),
            pltpu.VMEM((1024, C), F32),
            pltpu.VMEM((32, 32, C), BF16),
            pltpu.VMEM((2, 2, 32, C), BF16),
            pltpu.VMEM((2, 2, 32, C), BF16),
            pltpu.VMEM((2, 2, 32, C), BF16),
            pltpu.VMEM((2, 4, 16, C), BF16),
            pltpu.VMEM((2, 2304, 128), BF16),
            pltpu.VMEM((2304, 128), F32),
            pltpu.VMEM((2304, 128), BF16),
            pltpu.VMEM((2304, 128), BF16),
            pltpu.VMEM((3, 4, 192, 128), BF16),
            pltpu.VMEM((3, 192, 128), F32),
            pltpu.VMEM((3, 192, 128), BF16),
            pltpu.VMEM((3, 4, 48, 128), BF16),
            pltpu.VMEM((3, 4, 48, 128), BF16),
            pltpu.VMEM((2, 2304, 128), BF16),
            dma((2,)),
            dma((4, sends)),
            dma((4, sends)),
            dma((16,)),
            dma((16,)),
            dma((2, 8)),
            dma((2, 8)),
            dma((2,)),
            dma((2,)),
            dma((5, 3, 3)),
            dma((5, 3, 3)),
        ],
        compiler_params=pltpu.CompilerParams(
            collective_id=0, has_side_effects=True, vmem_limit_bytes=60 * 1024 * 1024
        ),
    )(
        box_class,
        box_offset,
        valid_count,
        feature_map,
        fpn_weight.reshape(2304, C),
        cot,
        head_weight.reshape(2304, C),
        deconv_weight.reshape(1024, C),
        mask_weight,
    )
    grad_weight = grad_weight.astype(F32).reshape(3, 3, C, C) / TOTAL
    return grad_input.reshape(32, 32, C), grad_weight


def solution(mesh):
    in_specs = (
        P("tile", "head", None),
        P(),
        P("head", None, None, None, None),
        P("head", None, None, None, None),
        P("head", None),
        P(("tile", "head")),
        P(("tile", "head"), None),
        P(("tile", "head")),
        P(("tile", "head"), None, None),
    )
    out_specs = (P("tile", "head", None), P())
    return jax.shard_map(local, mesh=mesh, in_specs=in_specs, out_specs=out_specs, check_vma=False)
```
